512 devices in a mesh: gx: 64 (over z_lo, y, core), yz: 8 (over x, z_hi).
Axes of the slice: x: 4, y: 8, z: 8 (z_hi: 2, z_lo: 4; z = z_hi * 4 + z_lo), core: 2. Of those that a mesh axis runs over, the one named last changes fastest.
Arguments:
- volume: bfloat16 [4, 256, 32, 256], P(None, 'gx', 'yz'), may hold values from -1200 to 1200
- weight_one: bfloat16 [3, 3, 3, 4, 16], replicated, may hold values from -0.625 to 0.625
- offset_one: float32 [16], replicated, may hold values from -3 to 3
- weight_two: bfloat16 [3, 3, 3, 16, 16], replicated, may hold values from -0.3125 to 0.3125
- offset_two: float32 [16], replicated, may hold values from -3 to 3
- weight_three: bfloat16 [3, 3, 3, 16, 32], replicated, may hold values from -0.3125 to 0.3125
- offset_three: float32 [32], replicated, may hold values from -3 to 3
- weight_four: bfloat16 [3, 3, 3, 32, 128], replicated, may hold values from -0.21875 to 0.21875
- offset_four: float32 [128], replicated, may hold values from -3 to 3
- weight_five: bfloat16 [3, 3, 3, 128, 128], replicated, may hold values from -0.109375 to 0.109375
- offset_five: float32 [128], replicated, may hold values from -3 to 3
- weight_up: bfloat16 [128, 32], replicated, may hold values from -0.5 to 0.5
Outputs:
- decoded: bfloat16 [32, 128, 16, 128], P(None, 'gx', 'yz')
The draws below stay inside these ranges and needn't reach their ends.
All inputs are finite; a program needn't handle non-finite values.
Results may differ from the reference program's by a relative error of at most 0.02.
Values may be sent and summed in bfloat16 or wider, within the bound.
No kernel may reach another device: no remote copies, remote signals or barrier semaphores. Data moves between devices by JAX's collectives and lax.ppermute only.
A program may use at most 64 MiB of HBM per device.

```python
import jax
import jax.numpy as jnp
from jax import lax

CIN = 4
C1 = 16
C2 = 32
C3 = 128
NZ = 256
NX = 256
NY = 32


def row_amplitude(key):
    power_key = jax.random.fold_in(key, 11)
    band_key = jax.random.fold_in(key, 13)
    exponents = jax.random.uniform(power_key, (NX,), jnp.float32, 0.0, 1.0)
    amplitude = jnp.power(10.0, exponents)
    band_width = min(8, NX)
    band_start = jax.random.randint(band_key, (), 0, NX - band_width + 1)
    rows_index = jnp.arange(NX, dtype=jnp.int32)
    inside = jnp.logical_and(rows_index >= band_start, rows_index < band_start + band_width)
    return amplitude * jnp.where(inside, 6.0, 1.0)


def draw_volume(key, part):
    key = jax.random.fold_in(key, 5)
    depth_scale = row_amplitude(key)
    chan_pos = jnp.arange(CIN, dtype=jnp.float32) / max(CIN - 1, 1)
    chan_scale = jnp.power(10.0, 0.5 * chan_pos)
    base = jnp.clip(jax.random.normal(key, (CIN, NX, NY, NZ), jnp.float32), -4.0, 4.0)
    field = base * chan_scale[:, None, None, None] * depth_scale[None, :, None, None]
    return field.astype(jnp.bfloat16)


def gaussian(stream_key, dims, spread, bound, kind=jnp.bfloat16):
    return jnp.clip(spread * jax.random.normal(stream_key, dims, jnp.float32), -bound, bound).astype(kind)


def setup_inputs(seed: int = 0) -> dict:
    splits = jax.random.split(jax.random.key(seed), 13)
    return {
        "volume": draw_volume(jax.random.fold_in(splits[12], 71), 0),
        "weight_one": gaussian(splits[1], (3, 3, 3, CIN, C1), (27 * CIN) ** -0.5, 0.625),
        "offset_one": gaussian(splits[2], (C1,), 0.5, 3.0, jnp.float32),
        "weight_two": gaussian(splits[3], (3, 3, 3, C1, C1), (27 * C1) ** -0.5, 0.3125),
        "offset_two": gaussian(splits[4], (C1,), 0.5, 3.0, jnp.float32),
        "weight_three": gaussian(splits[5], (3, 3, 3, C1, C2), (27 * C1) ** -0.5, 0.3125),
        "offset_three": gaussian(splits[6], (C2,), 0.5, 3.0, jnp.float32),
        "weight_four": gaussian(splits[7], (3, 3, 3, C2, C3), (27 * C2) ** -0.5, 0.21875),
        "offset_four": gaussian(splits[8], (C3,), 0.5, 3.0, jnp.float32),
        "weight_five": gaussian(splits[9], (3, 3, 3, C3, C3), (27 * C3) ** -0.5, 0.109375),
        "offset_five": gaussian(splits[10], (C3,), 0.5, 3.0, jnp.float32),
        "weight_up": gaussian(splits[11], (C3, C2), C3 ** -0.5, 0.5),
    }


epsilon = 1e-05

def convolve(field, kernel):
    result = lax.conv_general_dilated(field.astype(jnp.float32)[None], kernel.astype(jnp.float32), (1, 1, 1), ((1, 1), (1, 1), (1, 1)), dimension_numbers=('NCDHW', 'DHWIO', 'NCDHW'), precision=lax.Precision.HIGHEST)
    return result[0]

def standardize(value, offset):
    cells_total = value.shape[1] * value.shape[2] * value.shape[3]
    column_sum = lax.optimization_barrier(jnp.sum(value, axis=(1, 2, 3)))
    square_sum = lax.optimization_barrier(jnp.sum(value * value, axis=(1, 2, 3)))
    average = column_sum / cells_total
    variance = square_sum / cells_total - average * average
    inverse = lax.rsqrt(variance + epsilon)
    normed = (value - average[:, None, None, None]) * inverse[:, None, None, None] + offset[:, None, None, None]
    return jnp.maximum(normed, 0.0).astype(jnp.bfloat16)

def coarsen(active):
    shape = active.shape
    blocks = active.astype(jnp.float32).reshape(shape[0], shape[1] // 2, 2, shape[2] // 2, 2, shape[3] // 2, 2)
    return lax.optimization_barrier(jnp.mean(blocks, axis=(2, 4, 6))).astype(jnp.bfloat16)

def enlarge(field):
    return jnp.repeat(jnp.repeat(jnp.repeat(field, 2, axis=1), 2, axis=2), 2, axis=3)

def reference(volume, weight_one, offset_one, weight_two, offset_two, weight_three, offset_three, weight_four, offset_four, weight_five, offset_five, weight_up):
    first = standardize(convolve(volume, weight_one), offset_one)
    second = standardize(convolve(first, weight_two), offset_two)
    middle = standardize(convolve(coarsen(second), weight_three), offset_three)
    fourth = standardize(convolve(coarsen(middle), weight_four), offset_four)
    fifth = standardize(convolve(fourth, weight_five), offset_five)
    projected = jnp.einsum('cxyz,co->oxyz', fifth.astype(jnp.float32), weight_up.astype(jnp.float32))
    decoded = jnp.maximum(enlarge(projected) + middle.astype(jnp.float32), 0.0)
    return decoded.astype(jnp.bfloat16)
```

```python
import jax
import jax.numpy as jnp
from jax import lax
from jax.experimental import pallas as pl
from jax.experimental.pallas import tpu as pltpu
from jax.sharding import PartitionSpec as P

epsilon = 1e-05
f32 = jnp.float32
bf16 = jnp.bfloat16


def iota(shape, dim):
    return lax.broadcasted_iota(jnp.int32, shape, dim)


def tap_rows(kernel, before, slots):
    taps = jnp.transpose(kernel, (2, 4, 0, 1, 3)).astype(f32)
    taps = jnp.pad(taps, ((0, 0), (0, 0), (0, 0), (before, slots - 3 - before), (0, 0)))
    out, inner = kernel.shape[4], kernel.shape[3]
    taps = taps.reshape(3 * out, 3 * slots * inner)
    return jnp.pad(taps, ((0, 0), (0, -taps.shape[1] % 128)))


def fill_band(taps, band, step, out):
    depth = band.shape[1]
    base = taps[...]
    for row in range(8):
        moved = base if row == 0 else pltpu.roll(base, row * step, 1)
        for dz in range(3):
            start = (dz * 8 + row) * out
            band[start : start + out, :] = moved[dz * out : (dz + 1) * out, :depth].astype(bf16)


def merge_depth(parts, rows):
    width = parts.shape[1]
    lane = iota((rows, width), 1)
    before = jnp.where(lane == 0, 0.0, pltpu.roll(parts[:rows], 1, 1))
    after = jnp.where(lane == width - 1, 0.0, pltpu.roll(parts[2 * rows :], width - 1, 1))
    return parts[rows : 2 * rows] + before + after


def put_stats(stats, sums, squares):
    count = stats.shape[0]
    line = jnp.concatenate(
        [
            jnp.sum(sums.T, axis=0, keepdims=True),
            jnp.sum(squares.T, axis=0, keepdims=True),
        ],
        axis=0,
    )
    stats[...] = jnp.broadcast_to(line[None], (count, 2, 128))


def row_factors(stats, offset, channels, cells):
    total = jnp.sum(stats[...], axis=0)
    lane = iota((128, 128), 1)
    same = (iota((128, 128), 0) & (channels - 1)) == (lane & (channels - 1))

    def column(line, keep):
        return jnp.sum(jnp.where(keep, line, 0.0), axis=1, keepdims=True)

    average = column(total[0:1], same) / cells
    variance = column(total[1:2], same) / cells - average * average
    shift = column(offset[...], jnp.logical_and(same, lane < channels))
    return average, lax.rsqrt(variance + epsilon), shift


def lane_factors(stats, offset, cells):
    total = jnp.sum(stats[...], axis=0)
    average = total[0:1] / cells
    variance = total[1:2] / cells - average * average
    return average, lax.rsqrt(variance + epsilon), offset[...]


def normed(value, factors):
    average, inverse, shift = factors
    return jnp.maximum((value - average) * inverse + shift, 0.0)


def first_kernel(low, own, high, taps, value, stats, field, band, sums, squares):
    fill_band(taps, band, 4, 16)
    field[:, 0:16, :] = jnp.zeros((12, 16, 256), bf16)
    field[:, 144:160, :] = jnp.zeros((12, 16, 256), bf16)
    for place, part in enumerate((low, own, high)):
        for x in range(4):
            for block in range(8):
                field[place * 4 + x, 16 + 16 * block : 32 + 16 * block, :] = part[block, x]
    sums[...] = jnp.zeros_like(sums)
    squares[...] = jnp.zeros_like(squares)

    def step(x, carry):
        for group in range(4):
            window = jnp.concatenate(
                [field[x + dx, 32 * group : 32 * group + 64, :] for dx in range(3)], axis=0
            )
            parts = jnp.dot(band[...], window, preferred_element_type=f32)
            result = merge_depth(parts, 128)
            value[x, 128 * group : 128 * group + 128, :] = result

            @pl.when(jnp.logical_and(x >= 3, x < 7))
            def _():
                sums[...] += result[:, :128] + result[:, 128:]
                squares[...] += result[:, :128] * result[:, :128] + result[:, 128:] * result[:, 128:]

        return carry

    lax.fori_loop(0, 10, step, 0)
    put_stats(stats, sums[...], squares[...])


def second_kernel(
    count, place, raw, before, offset, taps, value, stats, field, band, sums, squares
):
    fill_band(taps, band, 16, 16)
    factors = row_factors(before, offset, 16, count * 4 * 32 * 256)
    field[:, 0:16, :] = jnp.zeros((10, 16, 256), bf16)
    field[:, 528:544, :] = jnp.zeros((10, 16, 256), bf16)
    sums[...] = jnp.zeros_like(sums)
    squares[...] = jnp.zeros_like(squares)
    start = place[0] * 4 - 3

    def prepare(x, carry):
        inside = jnp.logical_and(start + x >= 0, start + x < count * 4)
        for group in range(4):
            active = normed(raw[x, 128 * group : 128 * group + 128, :], factors)
            active = jnp.where(inside, active, 0.0).astype(bf16)
            field[x, 16 + 128 * group : 144 + 128 * group, :] = active
        return carry

    lax.fori_loop(0, 10, prepare, 0)

    def step(x, carry):
        for group in range(4):
            window = jnp.concatenate(
                [field[x + dx, 128 * group : 128 * group + 160, :] for dx in range(3)], axis=0
            )
            parts = jnp.dot(band[...], window, preferred_element_type=f32)
            result = merge_depth(parts, 128)
            value[x, 128 * group : 128 * group + 128, :] = result

            @pl.when(jnp.logical_and(x >= 2, x < 6))
            def _():
                sums[...] += result[:, :128] + result[:, 128:]
                squares[...] += result[:, :128] * result[:, :128] + result[:, 128:] * result[:, 128:]

        return carry

    lax.fori_loop(0, 8, step, 0)
    put_stats(stats, sums[...], squares[...])


def third_kernel(count, place, raw, before, offset, taps, value, stats, field, band):
    fill_band(taps, band, 16, 32)
    factors = row_factors(before, offset, 16, count * 4 * 32 * 256)
    halve = jnp.where((iota((256, 128), 0) >> 1) == iota((256, 128), 1), 0.125, 0.0).astype(bf16)
    field[:, 0:16, :] = jnp.zeros((4, 16, 128), bf16)
    field[:, 272:288, :] = jnp.zeros((4, 16, 128), bf16)
    start = place[0] * 2 - 1

    def prepare(x, carry):
        inside = jnp.logical_and(start + x >= 0, start + x < count * 2)
        for group in range(4):
            total = None
            for side in range(2):
                active = normed(raw[2 * x + side, 128 * group : 128 * group + 128, :], factors)
                part = jnp.dot(active.astype(bf16), halve, preferred_element_type=f32)
                total = part if total is None else total + part
            total = jnp.sum(total.reshape(4, 2, 16, 128), axis=1).reshape(64, 128)
            total = jnp.where(inside, total, 0.0).astype(bf16)
            field[x, 16 + 64 * group : 80 + 64 * group, :] = total
        return carry

    lax.fori_loop(0, 4, prepare, 0)
    sums = jnp.zeros((128, 128), f32)
    squares = jnp.zeros((128, 128), f32)
    for x in range(2):
        window = jnp.concatenate(
            [
                jnp.concatenate([field[x + dx, 128 * group : 128 * group + 160, :] for dx in range(3)], axis=0)
                for group in range(2)
            ],
            axis=1,
        )
        parts = jnp.dot(band[...], window, preferred_element_type=f32)
        for group in range(2):
            result = merge_depth(parts[:, 128 * group : 128 * group + 128], 256)
            value[x, 256 * group : 256 * group + 256, :] = result
            sums = sums + result[:128] + result[128:]
            squares = squares + result[:128] * result[:128] + result[128:] * result[128:]
    put_stats(stats, sums, squares)


def middle_kernel(count, raw, before, offset, middle, pooled):
    factors = row_factors(before, offset, 32, count * 2 * 16 * 128)
    for x in range(2):
        for group in range(4):
            active = normed(raw[x, 128 * group : 128 * group + 128, :], factors).astype(bf16)
            middle[x, 128 * group : 128 * group + 128, :] = active
    halve = jnp.where(((iota((64, 512), 1) & 127) >> 1) == iota((64, 512), 0), 0.125, 0.0).astype(bf16)
    for y in range(8):
        cells = jnp.concatenate(
            [middle[x, 64 * y + 32 * side : 64 * y + 32 * side + 32, :] for x in range(2) for side in range(2)],
            axis=1,
        )
        total = lax.dot_general(halve, cells, (((1,), (1,)), ((), ())), preferred_element_type=f32)
        pooled[64 * y : 64 * y + 64, :] = total.astype(bf16)


def along_depth(value):
    rows = value.shape[0]
    depth = iota(value.shape, 0) & 63
    before = jnp.where(depth == 0, 0.0, pltpu.roll(value, 1, 0))
    after = jnp.where(depth == 63, 0.0, pltpu.roll(value, rows - 1, 0))
    return before, value, after


def merge_side(parts):
    none = jnp.zeros((64, 128), f32)
    return (
        parts[:, 128:256]
        + jnp.concatenate([none, parts[:-64, 0:128]], axis=0)
        + jnp.concatenate([parts[64:, 256:384], none], axis=0)
    )


def put_lane_stats(stats, result):
    count = stats.shape[0]
    line = jnp.concatenate(
        [jnp.sum(result, axis=0, keepdims=True), jnp.sum(result * result, axis=0, keepdims=True)], axis=0
    )
    stats[...] = jnp.broadcast_to(line[None], (count, 2, 128))


def fourth_kernel(far_low, low, own, high, far_high, kernel, value, stats):
    taps = jnp.concatenate(
        [
            jnp.concatenate([kernel[dx * 9 + dy * 3 + dz] for dy in range(3)], axis=1)
            for dx in range(3)
            for dz in range(3)
        ],
        axis=0,
    )
    views = [
        [view.astype(bf16) for view in along_depth(part[...].astype(f32))]
        for part in (far_low, low, own, high, far_high)
    ]
    for x in range(3):
        window = jnp.concatenate([view for dx in range(3) for view in views[x + dx]], axis=1)
        parts = jnp.dot(window, taps, preferred_element_type=f32)
        result = merge_side(parts)
        value[x] = result
        if x == 1:
            put_lane_stats(stats, result)


def fifth_kernel(count, place, raw, before, offset, kernel, value, stats, field, taps):
    factors = lane_factors(before, offset, count * 8 * 64)
    for dx in range(3):
        for dz in range(3):
            row = (dx * 3 + dz) * 128
            for dy in range(3):
                taps[row : row + 128, dy * 128 : dy * 128 + 128] = kernel[dx * 9 + dy * 3 + dz]
    start = place[0] - 1
    for x in range(3):
        inside = jnp.logical_and(start + x >= 0, start + x < count)
        active = jnp.where(inside, normed(raw[x], factors), 0.0)
        for dz, view in enumerate(along_depth(active)):
            lane = (x * 3 + dz) * 128
            field[:, lane : lane + 128] = view.astype(bf16)
    parts = jnp.dot(field[...], taps[...], preferred_element_type=f32)
    result = merge_side(parts)
    value[...] = result
    put_lane_stats(stats, result)


def decode_kernel(count, place, raw, before, offset, up, middle, decoded):
    factors = lane_factors(before, offset, count * 8 * 64)
    stripe = place[0]
    active = normed(raw[pl.ds(pl.multiple_of(stripe * 64, 64), 64), :], factors).astype(bf16)
    twice = jnp.where((iota((128, 64), 0) >> 1) == iota((128, 64), 1), 1.0, 0.0).astype(bf16)
    active = jnp.dot(twice, active, preferred_element_type=f32).astype(bf16)
    projected = lax.dot_general(up[...], active, (((1,), (1,)), ((), ())), preferred_element_type=f32)
    blocks = []
    for x in range(2):
        own = middle[x, pl.ds(pl.multiple_of(stripe * 64, 64), 64), :].astype(f32)
        for side in range(2):
            merged = jnp.maximum(projected + own[32 * side : 32 * side + 32], 0.0)
            blocks.append(merged.astype(bf16))
    blocks = jnp.concatenate(blocks, axis=0)
    row = iota((128, 128), 0)
    order = jnp.where(((row & 3) * 32 + (row >> 2)) == iota((128, 128), 1), 1.0, 0.0).astype(bf16)
    decoded[...] = jnp.dot(order, blocks, preferred_element_type=f32).astype(bf16)


def shape(dims, kind=f32):
    return jax.ShapeDtypeStruct(dims, kind)


def call(kernel, outs, scratch=(), scalar=False, inputs=0, cost=0):
    specs = [pl.BlockSpec(memory_space=pltpu.VMEM)] * inputs
    if scalar:
        specs = [pl.BlockSpec(memory_space=pltpu.SMEM)] + specs
    return pl.pallas_call(
        kernel,
        out_shape=outs,
        in_specs=specs,
        out_specs=jax.tree.map(lambda _: pl.BlockSpec(memory_space=pltpu.VMEM), outs),
        scratch_shapes=list(scratch),
        compiler_params=pltpu.CompilerParams(vmem_limit_bytes=40 * 1024 * 1024),
        cost_estimate=pl.CostEstimate(flops=cost, bytes_accessed=1 << 20, transcendentals=0),
    )


def swap(stats):
    return lax.all_to_all(stats, "gx", 0, 0)


def bind(kernel, count):
    def bound(*refs):
        kernel(count, *refs)

    return bound


def shards(
    volume,
    weight_one,
    offset_one,
    weight_two,
    offset_two,
    weight_three,
    offset_three,
    weight_four,
    offset_four,
    weight_five,
    offset_five,
    weight_up,
):
    count = lax.axis_size("gx")
    place = lax.axis_index("gx").astype(jnp.int32)[None]
    stripe = lax.axis_index("yz").astype(jnp.int32)[None]

    def moved(block, by):
        pairs = [(i, i + by) for i in range(count) if 0 <= i + by < count]
        return lax.ppermute(block, "gx", pairs)

    def line(offset):
        return jnp.pad(offset, (0, 128 - offset.shape[0]))[None]

    statistics = shape((count, 2, 128))
    plane = pltpu.VMEM((128, 128), f32)

    block = jnp.transpose(volume, (1, 2, 0, 3)).reshape(4, 16, 256)
    own = lax.all_to_all(jnp.broadcast_to(block[None], (8, 4, 16, 256)), "yz", 0, 0)
    low, high = moved(own, 1), moved(own, -1)
    raw, stats = call(
        first_kernel,
        (shape((10, 512, 256)), statistics),
        (pltpu.VMEM((12, 160, 256), bf16), pltpu.VMEM((384, 192), bf16), plane, plane),
        inputs=4,
    )(low, own, high, tap_rows(weight_one, 3, 16))
    raw, stats = call(
        bind(second_kernel, count),
        (shape((8, 512, 256)), statistics),
        (pltpu.VMEM((10, 544, 256), bf16), pltpu.VMEM((384, 480), bf16), plane, plane),
        scalar=True,
        inputs=4,
    )(place, raw, swap(stats), line(offset_one), tap_rows(weight_two, 0, 10))
    raw, stats = call(
        bind(third_kernel, count),
        (shape((2, 512, 128)), statistics),
        (pltpu.VMEM((4, 288, 128), bf16), pltpu.VMEM((768, 480), bf16)),
        scalar=True,
        inputs=4,
    )(place, raw, swap(stats), line(offset_two), tap_rows(weight_three, 0, 10))
    middle, pooled = call(
        bind(middle_kernel, count),
        (shape((2, 512, 128), bf16), shape((512, 32), bf16)),
        inputs=3,
    )(raw, swap(stats), line(offset_three))
    raw, stats = call(
        fourth_kernel,
        (shape((3, 512, 128)), statistics),
        inputs=6,
    )(
        moved(pooled, 2),
        moved(pooled, 1),
        pooled,
        moved(pooled, -1),
        moved(pooled, -2),
        weight_four.reshape(27, 32, 128),
    )
    raw, stats = call(
        bind(fifth_kernel, count),
        (shape((512, 128)), statistics),
        (pltpu.VMEM((512, 1152), bf16), pltpu.VMEM((1152, 384), bf16)),
        scalar=True,
        inputs=4,
    )(place, raw, swap(stats), offset_four[None], weight_five.reshape(27, 128, 128))
    decoded = call(
        bind(decode_kernel, count),
        shape((128, 128), bf16),
        scalar=True,
        inputs=5,
    )(stripe, raw, swap(stats), offset_five[None], weight_up.T, middle)
    return decoded.reshape(32, 2, 2, 128)


def solution(mesh):
    return jax.shard_map(
        shards,
        mesh=mesh,
        in_specs=(P(None, "gx", "yz", None), P(), P(), P(), P(), P(), P(), P(), P(), P(), P(), P()),
        out_specs=P(None, "gx", "yz", None),
        check_vma=False,
    )
```

```python
import jax
import jax.numpy as jnp
from jax import lax
from jax.experimental import pallas as pl
from jax.experimental.pallas import tpu as pltpu
from jax.sharding import PartitionSpec as P

epsilon = 1e-05
f32 = jnp.float32
bf16 = jnp.bfloat16


def iota(shape, dim):
    return lax.broadcasted_iota(jnp.int32, shape, dim)


def tap_rows(kernel, before, slots):
    taps = jnp.transpose(kernel, (2, 4, 0, 1, 3)).astype(f32)
    taps = jnp.pad(taps, ((0, 0), (0, 0), (0, 0), (before, slots - 3 - before), (0, 0)))
    out, inner = kernel.shape[4], kernel.shape[3]
    taps = taps.reshape(3 * out, 3 * slots * inner)
    return jnp.pad(taps, ((0, 0), (0, -taps.shape[1] % 128)))


def fill_band(taps, band, step, out):
    depth = band.shape[1]
    base = taps[...]
    for row in range(8):
        moved = base if row == 0 else pltpu.roll(base, row * step, 1)
        for dz in range(3):
            start = (dz * 8 + row) * out
            band[start : start + out, :] = moved[dz * out : (dz + 1) * out, :depth].astype(bf16)


def merge_depth(parts, rows):
    width = parts.shape[1]
    lane = iota((rows, width), 1)
    before = jnp.where(lane == 0, 0.0, pltpu.roll(parts[:rows], 1, 1))
    after = jnp.where(lane == width - 1, 0.0, pltpu.roll(parts[2 * rows :], width - 1, 1))
    return parts[rows : 2 * rows] + before + after


def put_stats(stats, sums, squares):
    count = stats.shape[0]
    none = jnp.zeros((128 - sums.shape[0], 128), f32)
    lines = [
        jnp.sum(jnp.concatenate([part, none], axis=0).T, axis=0, keepdims=True) for part in (sums, squares)
    ]
    stats[...] = jnp.broadcast_to(jnp.concatenate(lines, axis=0)[None], (count, 2, 128))


def folded(value, channels):
    width = value.shape[1]
    total = value[:, :128]
    for start in range(128, width, 128):
        total = total + value[:, start : start + 128]
    return jnp.sum(total.reshape(-1, channels, 128), axis=0)


def row_factors(stats, offset, channels, cells):
    total = jnp.sum(stats[...], axis=0)
    lane = iota((128, 128), 1)
    same = (iota((128, 128), 0) & (channels - 1)) == (lane & (channels - 1))

    def column(line, keep):
        return jnp.sum(jnp.where(keep, line, 0.0), axis=1, keepdims=True)

    average = column(total[0:1], same) / cells
    variance = column(total[1:2], same) / cells - average * average
    shift = column(offset[...], jnp.logical_and(same, lane < channels))
    return average, lax.rsqrt(variance + epsilon), shift


def lane_factors(stats, offset, cells):
    total = jnp.sum(stats[...], axis=0)
    average = total[0:1] / cells
    variance = total[1:2] / cells - average * average
    return average, lax.rsqrt(variance + epsilon), offset[...]


def normed(value, factors):
    average, inverse, shift = factors
    return jnp.maximum((value - average) * inverse + shift, 0.0)


def load_rows(source, target, arrived, rows):
    copies = [pltpu.make_async_copy(source.at[x], target.at[x], arrived.at[x]) for x in rows]
    for copy in copies:
        copy.start()
    return copies


def put_volume(low, own, high, field, rows):
    for x in rows:
        field[x, 0:16, :] = jnp.zeros((16, 256), bf16)
        field[x, 144:160, :] = jnp.zeros((16, 256), bf16)
        part = (low, own, high)[x // 4]
        for block in range(8):
            field[x, 16 + 16 * block : 32 + 16 * block, :] = part[block, x % 4]


def first_block(field, band, x, group):
    window = jnp.concatenate(
        [field[x + dx, 32 * group : 32 * group + 64, :] for dx in range(3)], axis=0
    )
    return merge_depth(jnp.dot(band[...], window, preferred_element_type=f32), 128)


def second_block(field, band, x, group):
    window = jnp.concatenate(
        [field[x + dx, 128 * group : 128 * group + 160, :] for dx in range(3)], axis=0
    )
    return merge_depth(jnp.dot(band[...], window, preferred_element_type=f32), 128)


def sum_rows(block, field, band, stats, begin, end):
    def step(x, carry):
        sums, squares = carry
        for group in range(4):
            result = block(field, band, x, group)
            sums = sums + folded(result, 16)
            squares = squares + folded(result * result, 16)
        return sums, squares

    none = jnp.zeros((16, 128), f32)
    sums, squares = lax.fori_loop(begin, end, step, (none, none), unroll=2)
    put_stats(stats, sums, squares)


def write_rows(block, field, band, value, staged, left):
    count = value.shape[0]

    def step(x, carry):
        for group in range(4):
            staged[x, 128 * group : 128 * group + 128, :] = block(field, band, x, group)
        pltpu.make_async_copy(staged.at[x], value.at[x], left.at[x]).start()
        return carry

    def finish(x, carry):
        pltpu.make_async_copy(staged.at[x], value.at[x], left.at[x]).wait()
        return carry

    lax.fori_loop(0, count, step, 0)
    lax.fori_loop(0, count, finish, 0)


def first_sums_kernel(low, own, high, taps, stats, field, band):
    fill_band(taps, band, 4, 16)
    put_volume(low, own, high, field, range(3, 9))
    sum_rows(first_block, field, band, stats, 3, 7)


def first_rows_kernel(low, own, high, taps, value, field, band, staged, left):
    fill_band(taps, band, 4, 16)
    put_volume(low, own, high, field, range(12))
    write_rows(first_block, field, band, value, staged, left)


def put_first(count, place, source, raw, arrived, before, offset, field, begin, end):
    copies = load_rows(source, raw, arrived, range(begin, end))
    factors = row_factors(before, offset, 16, count * 4 * 32 * 256)
    start = place[0] * 4 - 3
    for x in range(begin, end):
        copies[x - begin].wait()
        inside = jnp.logical_and(start + x >= 0, start + x < count * 4)
        field[x, 0:16, :] = jnp.zeros((16, 256), bf16)
        field[x, 528:544, :] = jnp.zeros((16, 256), bf16)
        for group in range(4):
            active = normed(raw[x, 128 * group : 128 * group + 128, :], factors)
            active = jnp.where(inside, active, 0.0).astype(bf16)
            field[x, 16 + 128 * group : 144 + 128 * group, :] = active


def second_sums_kernel(
    count, place, source, before, offset, taps, stats, raw, arrived, field, band
):
    fill_band(taps, band, 16, 16)
    put_first(count, place, source, raw, arrived, before, offset, field, 2, 8)
    sum_rows(second_block, field, band, stats, 2, 6)


def second_rows_kernel(
    count, place, source, before, offset, taps, value, raw, arrived, field, band, staged, left
):
    fill_band(taps, band, 16, 16)
    put_first(count, place, source, raw, arrived, before, offset, field, 0, 10)
    write_rows(second_block, field, band, value, staged, left)


def third_kernel(count, place, source, before, offset, taps, value, stats, raw, arrived, field, band):
    copies = load_rows(source, raw, arrived, range(8))
    fill_band(taps, band, 16, 32)
    factors = row_factors(before, offset, 16, count * 4 * 32 * 256)
    halve = jnp.where((iota((256, 128), 0) >> 1) == iota((256, 128), 1), 0.125, 0.0).astype(bf16)
    start = place[0] * 2 - 1
    for x in range(4):
        copies[2 * x].wait()
        copies[2 * x + 1].wait()
        inside = jnp.logical_and(start + x >= 0, start + x < count * 2)
        field[x, 0:16, :] = jnp.zeros((16, 128), bf16)
        field[x, 272:288, :] = jnp.zeros((16, 128), bf16)
        for group in range(4):
            total = None
            for side in range(2):
                active = normed(raw[2 * x + side, 128 * group : 128 * group + 128, :], factors)
                part = jnp.dot(active.astype(bf16), halve, preferred_element_type=f32)
                total = part if total is None else total + part
            total = jnp.sum(total.reshape(4, 2, 16, 128), axis=1).reshape(64, 128)
            total = jnp.where(inside, total, 0.0).astype(bf16)
            field[x, 16 + 64 * group : 80 + 64 * group, :] = total
    sums = jnp.zeros((32, 128), f32)
    squares = jnp.zeros((32, 128), f32)
    for x in range(2):
        window = jnp.concatenate(
            [
                jnp.concatenate([field[x + dx, 128 * group : 128 * group + 160, :] for dx in range(3)], axis=0)
                for group in range(2)
            ],
            axis=1,
        )
        parts = jnp.dot(band[...], window, preferred_element_type=f32)
        for group in range(2):
            result = merge_depth(parts[:, 128 * group : 128 * group + 128], 256)
            value[x, 256 * group : 256 * group + 256, :] = result
            sums = sums + folded(result, 32)
            squares = squares + folded(result * result, 32)
    put_stats(stats, sums, squares)


def middle_kernel(count, raw, before, offset, middle, pooled):
    factors = row_factors(before, offset, 32, count * 2 * 16 * 128)
    for x in range(2):
        for group in range(4):
            active = normed(raw[x, 128 * group : 128 * group + 128, :], factors).astype(bf16)
            middle[x, 128 * group : 128 * group + 128, :] = active
    halve = jnp.where(((iota((64, 512), 1) & 127) >> 1) == iota((64, 512), 0), 0.125, 0.0).astype(bf16)
    for y in range(8):
        cells = jnp.concatenate(
            [middle[x, 64 * y + 32 * side : 64 * y + 32 * side + 32, :] for x in range(2) for side in range(2)],
            axis=1,
        )
        total = lax.dot_general(halve, cells, (((1,), (1,)), ((), ())), preferred_element_type=f32)
        pooled[64 * y : 64 * y + 64, :] = total.astype(bf16)


def along_depth(value):
    rows = value.shape[0]
    depth = iota(value.shape, 0) & 63
    before = jnp.where(depth == 0, 0.0, pltpu.roll(value, 1, 0))
    after = jnp.where(depth == 63, 0.0, pltpu.roll(value, rows - 1, 0))
    return before, value, after


def merge_side(parts):
    none = jnp.zeros((64, 128), f32)
    return (
        parts[:, 128:256]
        + jnp.concatenate([none, parts[:-64, 0:128]], axis=0)
        + jnp.concatenate([parts[64:, 256:384], none], axis=0)
    )


def put_lane_stats(stats, result):
    count = stats.shape[0]
    line = jnp.concatenate(
        [jnp.sum(result, axis=0, keepdims=True), jnp.sum(result * result, axis=0, keepdims=True)], axis=0
    )
    stats[...] = jnp.broadcast_to(line[None], (count, 2, 128))


def fourth_kernel(low, own, high, kernel, value, stats):
    taps = jnp.concatenate(
        [
            jnp.concatenate([kernel[dx * 9 + dy * 3 + dz] for dy in range(3)], axis=1)
            for dx in range(3)
            for dz in range(3)
        ],
        axis=0,
    )
    window = jnp.concatenate(
        [view.astype(bf16) for part in (low, own, high) for view in along_depth(part[...].astype(f32))], axis=1
    )
    result = merge_side(jnp.dot(window, taps, preferred_element_type=f32))
    value[...] = result
    put_lane_stats(stats, result)


def copy_kernel(value, copied):
    copied[...] = value[...]


def fifth_kernel(count, place, low, own, high, before, offset, kernel, value, stats, field, taps):
    factors = lane_factors(before, offset, count * 8 * 64)
    for dx in range(3):
        for dz in range(3):
            row = (dx * 3 + dz) * 128
            for dy in range(3):
                taps[row : row + 128, dy * 128 : dy * 128 + 128] = kernel[dx * 9 + dy * 3 + dz]
    start = place[0] - 1
    for x, part in enumerate((low, own, high)):
        inside = jnp.logical_and(start + x >= 0, start + x < count)
        active = jnp.where(inside, normed(part[...], factors), 0.0)
        for dz, view in enumerate(along_depth(active)):
            lane = (x * 3 + dz) * 128
            field[:, lane : lane + 128] = view.astype(bf16)
    parts = jnp.dot(field[...], taps[...], preferred_element_type=f32)
    result = merge_side(parts)
    value[...] = result
    put_lane_stats(stats, result)


def decode_kernel(count, place, raw, before, offset, up, middle, decoded):
    factors = lane_factors(before, offset, count * 8 * 64)
    stripe = place[0]
    active = normed(raw[pl.ds(pl.multiple_of(stripe * 64, 64), 64), :], factors).astype(bf16)
    twice = jnp.where((iota((128, 64), 0) >> 1) == iota((128, 64), 1), 1.0, 0.0).astype(bf16)
    active = jnp.dot(twice, active, preferred_element_type=f32).astype(bf16)
    projected = lax.dot_general(up[...], active, (((1,), (1,)), ((), ())), preferred_element_type=f32)
    blocks = []
    for x in range(2):
        own = middle[x, pl.ds(pl.multiple_of(stripe * 64, 64), 64), :].astype(f32)
        for side in range(2):
            merged = jnp.maximum(projected + own[32 * side : 32 * side + 32], 0.0)
            blocks.append(merged.astype(bf16))
    blocks = jnp.concatenate(blocks, axis=0)
    row = iota((128, 128), 0)
    order = jnp.where(((row & 3) * 32 + (row >> 2)) == iota((128, 128), 1), 1.0, 0.0).astype(bf16)
    decoded[...] = jnp.dot(order, blocks, preferred_element_type=f32).astype(bf16)


def shape(dims, kind=f32):
    return jax.ShapeDtypeStruct(dims, kind)


def call(kernel, outs, places, scratch=(), out_places=None):
    spaces = {"S": pltpu.SMEM, "V": pltpu.VMEM, "H": pltpu.HBM}

    def specs(letters):
        return tuple(pl.BlockSpec(memory_space=spaces[letter]) for letter in letters)

    single = not isinstance(outs, tuple)
    out_specs = specs(out_places or "V" * (1 if single else len(outs)))
    return pl.pallas_call(
        kernel,
        out_shape=outs,
        in_specs=specs(places),
        out_specs=out_specs[0] if single else out_specs,
        scratch_shapes=list(scratch),
        compiler_params=pltpu.CompilerParams(vmem_limit_bytes=28 * 1024 * 1024),
        cost_estimate=pl.CostEstimate(flops=1 << 30, bytes_accessed=1 << 22, transcendentals=0),
    )


def swap(stats):
    return lax.all_to_all(stats, "gx", 0, 0)


def bind(kernel, count):
    def bound(*refs):
        kernel(count, *refs)

    return bound


def shards(
    volume,
    weight_one,
    offset_one,
    weight_two,
    offset_two,
    weight_three,
    offset_three,
    weight_four,
    offset_four,
    weight_five,
    offset_five,
    weight_up,
):
    count = lax.axis_size("gx")
    place = lax.axis_index("gx").astype(jnp.int32)[None]
    stripe = lax.axis_index("yz").astype(jnp.int32)[None]

    def moved(block, by):
        pairs = [(i, i + by) for i in range(count) if 0 <= i + by < count]
        return lax.ppermute(block, "gx", pairs)

    def line(offset):
        return jnp.pad(offset, (0, 128 - offset.shape[0]))[None]

    statistics = shape((count, 2, 128))
    arrivals = pltpu.SemaphoreType.DMA
    taps_one = tap_rows(weight_one, 3, 16)
    taps_two = tap_rows(weight_two, 0, 10)

    block = jnp.transpose(volume, (1, 2, 0, 3)).reshape(4, 16, 256)
    own = lax.all_to_all(jnp.broadcast_to(block[None], (8, 4, 16, 256)), "yz", 0, 0)
    low, high = moved(own, 1), moved(own, -1)
    field = (pltpu.VMEM((12, 160, 256), bf16), pltpu.VMEM((384, 192), bf16))
    stats = call(first_sums_kernel, statistics, "VVVV", field)(low, own, high, taps_one)
    raw = call(
        first_rows_kernel,
        shape((10, 512, 256)),
        "VVVV",
        (*field, pltpu.VMEM((10, 512, 256), f32), arrivals((10,))),
        "H",
    )(low, own, high, taps_one)

    inputs = (place, raw, swap(stats), line(offset_one), taps_two)
    field = (
        pltpu.VMEM((10, 512, 256), f32),
        arrivals((10,)),
        pltpu.VMEM((10, 544, 256), bf16),
        pltpu.VMEM((384, 480), bf16),
    )
    stats = call(bind(second_sums_kernel, count), statistics, "SHVVV", field)(*inputs)
    raw = call(
        bind(second_rows_kernel, count),
        shape((8, 512, 256)),
        "SHVVV",
        (*field, pltpu.VMEM((8, 512, 256), f32), arrivals((8,))),
        "H",
    )(*inputs)

    raw, stats = call(
        bind(third_kernel, count),
        (shape((2, 512, 128)), statistics),
        "SHVVV",
        (
            pltpu.VMEM((8, 512, 256), f32),
            arrivals((8,)),
            pltpu.VMEM((4, 288, 128), bf16),
            pltpu.VMEM((768, 480), bf16),
        ),
    )(place, raw, swap(stats), line(offset_two), tap_rows(weight_three, 0, 10))

    middle, pooled = call(
        bind(middle_kernel, count),
        (shape((2, 512, 128), bf16), shape((512, 32), bf16)),
        "VVV",
    )(raw, swap(stats), line(offset_three))
    raw, stats = call(
        fourth_kernel,
        (shape((512, 128)), statistics),
        "VVVV",
    )(moved(pooled, 1), pooled, moved(pooled, -1), weight_four.reshape(27, 32, 128))

    sent = call(copy_kernel, shape((512, 128)), "V")(raw)
    raw, stats = call(
        bind(fifth_kernel, count),
        (shape((512, 128)), statistics),
        "SVVVVVV",
        (pltpu.VMEM((512, 1152), bf16), pltpu.VMEM((1152, 384), bf16)),
    )(
        place,
        moved(sent, 1),
        raw,
        moved(sent, -1),
        swap(stats),
        offset_four[None],
        weight_five.reshape(27, 128, 128),
    )
    decoded = call(
        bind(decode_kernel, count),
        shape((128, 128), bf16),
        "SVVVVV",
    )(stripe, raw, swap(stats), offset_five[None], weight_up.T, middle)
    return decoded.reshape(32, 2, 2, 128)


def solution(mesh):
    return jax.shard_map(
        shards,
        mesh=mesh,
        in_specs=(P(None, "gx", "yz", None), P(), P(), P(), P(), P(), P(), P(), P(), P(), P(), P()),
        out_specs=P(None, "gx", "yz", None),
        check_vma=False,
    )
```

```python
import jax
import jax.numpy as jnp
from jax import lax
from jax.experimental import pallas as pl
from jax.experimental.pallas import tpu as pltpu
from jax.sharding import PartitionSpec as P

epsilon = 1e-05
f32 = jnp.float32
bf16 = jnp.bfloat16


def iota(shape, dim):
    return lax.broadcasted_iota(jnp.int32, shape, dim)


def tap_rows(kernel, before, slots):
    taps = jnp.transpose(kernel, (2, 4, 0, 1, 3)).astype(f32)
    taps = jnp.pad(taps, ((0, 0), (0, 0), (0, 0), (before, slots - 3 - before), (0, 0)))
    out, inner = kernel.shape[4], kernel.shape[3]
    taps = taps.reshape(3 * out, 3 * slots * inner)
    return jnp.pad(taps, ((0, 0), (0, -taps.shape[1] % 128)))


def fill_band(taps, band, step, out):
    depth = band.shape[1]
    base = taps[...]
    for row in range(8):
        moved = base if row == 0 else pltpu.roll(base, row * step, 1)
        for dz in range(3):
            start = (dz * 8 + row) * out
            band[start : start + out, :] = moved[dz * out : (dz + 1) * out, :depth].astype(bf16)


def merge_depth(parts, rows):
    width = parts.shape[1]
    lane = iota((rows, width), 1)
    before = jnp.where(lane == 0, 0.0, pltpu.roll(parts[:rows], 1, 1))
    after = jnp.where(lane == width - 1, 0.0, pltpu.roll(parts[2 * rows :], width - 1, 1))
    return parts[rows : 2 * rows] + before + after


def put_stats(stats, sums, squares):
    count = stats.shape[0]
    none = jnp.zeros((128 - sums.shape[0], 128), f32)
    lines = [
        jnp.sum(jnp.concatenate([part, none], axis=0).T, axis=0, keepdims=True) for part in (sums, squares)
    ]
    stats[...] = jnp.broadcast_to(jnp.concatenate(lines, axis=0)[None], (count, 2, 128))


def folded(value, channels):
    width = value.shape[1]
    total = value[:, :128]
    for start in range(128, width, 128):
        total = total + value[:, start : start + 128]
    return jnp.sum(total.reshape(-1, channels, 128), axis=0)


def row_factors(stats, offset, channels, cells):
    total = jnp.sum(stats[...], axis=0)
    lane = iota((128, 128), 1)
    same = (iota((128, 128), 0) & (channels - 1)) == (lane & (channels - 1))

    def column(line, keep):
        return jnp.sum(jnp.where(keep, line, 0.0), axis=1, keepdims=True)

    average = column(total[0:1], same) / cells
    variance = column(total[1:2], same) / cells - average * average
    shift = column(offset[...], jnp.logical_and(same, lane < channels))
    return average, lax.rsqrt(variance + epsilon), shift


def lane_factors(stats, offset, cells):
    total = jnp.sum(stats[...], axis=0)
    average = total[0:1] / cells
    variance = total[1:2] / cells - average * average
    return average, lax.rsqrt(variance + epsilon), offset[...]


def normed(value, factors):
    average, inverse, shift = factors
    return jnp.maximum((value - average) * inverse + shift, 0.0)


def load_rows(source, target, arrived, rows):
    copies = [pltpu.make_async_copy(source.at[x], target.at[x], arrived.at[x]) for x in rows]
    for copy in copies:
        copy.start()
    return copies


def put_volume(low, own, high, field, rows):
    for x in rows:
        field[x, 0:16, :] = jnp.zeros((16, 256), bf16)
        field[x, 144:160, :] = jnp.zeros((16, 256), bf16)
        part = (low, own, high)[x // 4]
        for block in range(8):
            field[x, 16 + 16 * block : 32 + 16 * block, :] = part[block, x % 4]


def first_block(field, band, x, group):
    window = jnp.concatenate(
        [field[x + dx, 32 * group : 32 * group + 64, :] for dx in range(3)], axis=0
    )
    return merge_depth(jnp.dot(band[...], window, preferred_element_type=f32), 128)


def second_block(field, band, x, group):
    window = jnp.concatenate(
        [field[x + dx, 128 * group : 128 * group + 160, :] for dx in range(3)], axis=0
    )
    return merge_depth(jnp.dot(band[...], window, preferred_element_type=f32), 128)


def sum_rows(block, field, band, stats, begin, end):
    def step(x, carry):
        sums, squares = carry
        for group in range(4):
            result = block(field, band, x, group)
            sums = sums + folded(result, 16)
            squares = squares + folded(result * result, 16)
        return sums, squares

    none = jnp.zeros((16, 128), f32)
    sums, squares = lax.fori_loop(begin, end, step, (none, none), unroll=2)
    put_stats(stats, sums, squares)


def write_rows(block, field, band, value, staged, left):
    count = value.shape[0]

    def step(x, carry):
        for group in range(4):
            staged[x, 128 * group : 128 * group + 128, :] = block(field, band, x, group)
        pltpu.make_async_copy(staged.at[x], value.at[x], left.at[x]).start()
        return carry

    def finish(x, carry):
        pltpu.make_async_copy(staged.at[x], value.at[x], left.at[x]).wait()
        return carry

    lax.fori_loop(0, count, step, 0)
    lax.fori_loop(0, count, finish, 0)


def first_sums_kernel(low, own, high, taps, stats, field, band):
    fill_band(taps, band, 4, 16)
    put_volume(low, own, high, field, range(3, 9))
    sum_rows(first_block, field, band, stats, 3, 7)


def first_rows_kernel(low, own, high, taps, value, field, band, staged, left):
    fill_band(taps, band, 4, 16)
    put_volume(low, own, high, field, range(12))
    write_rows(first_block, field, band, value, staged, left)


def put_first(count, place, source, raw, arrived, before, offset, field, begin, end):
    copies = load_rows(source, raw, arrived, range(begin, end))
    factors = row_factors(before, offset, 16, count * 4 * 32 * 256)
    start = place[0] * 4 - 3
    for x in range(begin, end):
        copies[x - begin].wait()
        inside = jnp.logical_and(start + x >= 0, start + x < count * 4)
        field[x, 0:16, :] = jnp.zeros((16, 256), bf16)
        field[x, 528:544, :] = jnp.zeros((16, 256), bf16)
        for group in range(4):
            active = normed(raw[x, 128 * group : 128 * group + 128, :], factors)
            active = jnp.where(inside, active, 0.0).astype(bf16)
            field[x, 16 + 128 * group : 144 + 128 * group, :] = active


def second_sums_kernel(
    count, place, source, before, offset, taps, stats, raw, arrived, field, band
):
    fill_band(taps, band, 16, 16)
    put_first(count, place, source, raw, arrived, before, offset, field, 2, 8)
    sum_rows(second_block, field, band, stats, 2, 6)


def second_rows_kernel(
    count, place, source, before, offset, taps, value, raw, arrived, field, band, staged, left
):
    fill_band(taps, band, 16, 16)
    put_first(count, place, source, raw, arrived, before, offset, field, 0, 10)
    write_rows(second_block, field, band, value, staged, left)


def third_kernel(count, place, source, before, offset, taps, value, stats, raw, arrived, field, band):
    copies = load_rows(source, raw, arrived, range(8))
    fill_band(taps, band, 16, 32)
    factors = row_factors(before, offset, 16, count * 4 * 32 * 256)
    halve = jnp.where((iota((256, 128), 0) >> 1) == iota((256, 128), 1), 0.125, 0.0).astype(bf16)
    start = place[0] * 2 - 1
    for x in range(4):
        copies[2 * x].wait()
        copies[2 * x + 1].wait()
        inside = jnp.logical_and(start + x >= 0, start + x < count * 2)
        field[x, 0:16, :] = jnp.zeros((16, 128), bf16)
        field[x, 272:288, :] = jnp.zeros((16, 128), bf16)
        for group in range(4):
            total = None
            for side in range(2):
                active = normed(raw[2 * x + side, 128 * group : 128 * group + 128, :], factors)
                part = jnp.dot(active.astype(bf16), halve, preferred_element_type=f32)
                total = part if total is None else total + part
            total = jnp.sum(total.reshape(4, 2, 16, 128), axis=1).reshape(64, 128)
            total = jnp.where(inside, total, 0.0).astype(bf16)
            field[x, 16 + 64 * group : 80 + 64 * group, :] = total
    sums = jnp.zeros((32, 128), f32)
    squares = jnp.zeros((32, 128), f32)
    for x in range(2):
        window = jnp.concatenate(
            [
                jnp.concatenate([field[x + dx, 128 * group : 128 * group + 160, :] for dx in range(3)], axis=0)
                for group in range(2)
            ],
            axis=1,
        )
        parts = jnp.dot(band[...], window, preferred_element_type=f32)
        for group in range(2):
            result = merge_depth(parts[:, 128 * group : 128 * group + 128], 256)
            value[x, 256 * group : 256 * group + 256, :] = result
            sums = sums + folded(result, 32)
            squares = squares + folded(result * result, 32)
    put_stats(stats, sums, squares)


def middle_kernel(count, raw, before, offset, middle, pooled):
    factors = row_factors(before, offset, 32, count * 2 * 16 * 128)
    for x in range(2):
        for group in range(4):
            active = normed(raw[x, 128 * group : 128 * group + 128, :], factors).astype(bf16)
            middle[x, 128 * group : 128 * group + 128, :] = active
    halve = jnp.where(((iota((64, 512), 1) & 127) >> 1) == iota((64, 512), 0), 0.125, 0.0).astype(bf16)
    for y in range(8):
        cells = jnp.concatenate(
            [middle[x, 64 * y + 32 * side : 64 * y + 32 * side + 32, :] for x in range(2) for side in range(2)],
            axis=1,
        )
        total = lax.dot_general(halve, cells, (((1,), (1,)), ((), ())), preferred_element_type=f32)
        pooled[64 * y : 64 * y + 64, :] = total.astype(bf16)


def along_depth(value):
    rows = value.shape[0]
    depth = iota(value.shape, 0) & 63
    before = jnp.where(depth == 0, 0.0, pltpu.roll(value, 1, 0))
    after = jnp.where(depth == 63, 0.0, pltpu.roll(value, rows - 1, 0))
    return before, value, after


def merge_side(parts):
    none = jnp.zeros((64, 128), f32)
    return (
        parts[:, 128:256]
        + jnp.concatenate([none, parts[:-64, 0:128]], axis=0)
        + jnp.concatenate([parts[64:, 256:384], none], axis=0)
    )


def put_lane_stats(stats, result):
    count = stats.shape[0]
    line = jnp.concatenate(
        [jnp.sum(result, axis=0, keepdims=True), jnp.sum(result * result, axis=0, keepdims=True)], axis=0
    )
    stats[...] = jnp.broadcast_to(line[None], (count, 2, 128))


def fourth_row(parts, kernel):
    taps = jnp.concatenate(
        [
            jnp.concatenate([kernel[dx * 9 + dy * 3 + dz] for dy in range(3)], axis=1)
            for dx in range(3)
            for dz in range(3)
        ],
        axis=0,
    )
    window = jnp.concatenate(
        [view.astype(bf16) for part in parts for view in along_depth(part[...].astype(f32))], axis=1
    )
    return merge_side(jnp.dot(window, taps, preferred_element_type=f32))


def fourth_kernel(low, own, high, kernel, value, stats, pass_low, pass_high):
    result = fourth_row((low, own, high), kernel)
    value[...] = result
    put_lane_stats(stats, result)
    pass_low[...] = low[...]
    pass_high[...] = high[...]


def fifth_kernel(
    count, place, far_low, low, near, high, far_high, own, before, offset, kernel_four, kernel, value, stats, field, taps
):
    parts = (
        fourth_row((far_low, low, near), kernel_four),
        own[...],
        fourth_row((near, high, far_high), kernel_four),
    )
    factors = lane_factors(before, offset, count * 8 * 64)
    for dx in range(3):
        for dz in range(3):
            row = (dx * 3 + dz) * 128
            for dy in range(3):
                taps[row : row + 128, dy * 128 : dy * 128 + 128] = kernel[dx * 9 + dy * 3 + dz]
    start = place[0] - 1
    for x, part in enumerate(parts):
        inside = jnp.logical_and(start + x >= 0, start + x < count)
        active = jnp.where(inside, normed(part, factors), 0.0)
        for dz, view in enumerate(along_depth(active)):
            lane = (x * 3 + dz) * 128
            field[:, lane : lane + 128] = view.astype(bf16)
    parts = jnp.dot(field[...], taps[...], preferred_element_type=f32)
    result = merge_side(parts)
    value[...] = result
    put_lane_stats(stats, result)


def decode_kernel(count, place, raw, before, offset, up, middle, decoded):
    factors = lane_factors(before, offset, count * 8 * 64)
    stripe = place[0]
    active = normed(raw[pl.ds(pl.multiple_of(stripe * 64, 64), 64), :], factors).astype(bf16)
    twice = jnp.where((iota((128, 64), 0) >> 1) == iota((128, 64), 1), 1.0, 0.0).astype(bf16)
    active = jnp.dot(twice, active, preferred_element_type=f32).astype(bf16)
    projected = lax.dot_general(up[...], active, (((1,), (1,)), ((), ())), preferred_element_type=f32)
    blocks = []
    for x in range(2):
        own = middle[x, pl.ds(pl.multiple_of(stripe * 64, 64), 64), :].astype(f32)
        for side in range(2):
            merged = jnp.maximum(projected + own[32 * side : 32 * side + 32], 0.0)
            blocks.append(merged.astype(bf16))
    blocks = jnp.concatenate(blocks, axis=0)
    row = iota((128, 128), 0)
    order = jnp.where(((row & 3) * 32 + (row >> 2)) == iota((128, 128), 1), 1.0, 0.0).astype(bf16)
    decoded[...] = jnp.dot(order, blocks, preferred_element_type=f32).astype(bf16)


def shape(dims, kind=f32):
    return jax.ShapeDtypeStruct(dims, kind)


def call(kernel, outs, places, scratch=(), out_places=None, grant=28):
    spaces = {"S": pltpu.SMEM, "V": pltpu.VMEM, "H": pltpu.HBM}

    def specs(letters):
        return tuple(pl.BlockSpec(memory_space=spaces[letter]) for letter in letters)

    single = not isinstance(outs, tuple)
    out_specs = specs(out_places or "V" * (1 if single else len(outs)))
    return pl.pallas_call(
        kernel,
        out_shape=outs,
        in_specs=specs(places),
        out_specs=out_specs[0] if single else out_specs,
        scratch_shapes=list(scratch),
        compiler_params=pltpu.CompilerParams(vmem_limit_bytes=grant * 1024 * 1024),
        cost_estimate=pl.CostEstimate(flops=1 << 30, bytes_accessed=1 << 22, transcendentals=0),
    )


def swap(stats):
    return lax.all_to_all(stats, "gx", 0, 0)


def bind(kernel, count):
    def bound(*refs):
        kernel(count, *refs)

    return bound


def shards(
    volume,
    weight_one,
    offset_one,
    weight_two,
    offset_two,
    weight_three,
    offset_three,
    weight_four,
    offset_four,
    weight_five,
    offset_five,
    weight_up,
):
    count = lax.axis_size("gx")
    place = lax.axis_index("gx").astype(jnp.int32)[None]
    stripe = lax.axis_index("yz").astype(jnp.int32)[None]

    def moved(block, by):
        pairs = [(i, i + by) for i in range(count) if 0 <= i + by < count]
        return lax.ppermute(block, "gx", pairs)

    def line(offset):
        return jnp.pad(offset, (0, 128 - offset.shape[0]))[None]

    statistics = shape((count, 2, 128))
    large = 51
    arrivals = pltpu.SemaphoreType.DMA
    taps_one = tap_rows(weight_one, 3, 16)
    taps_two = tap_rows(weight_two, 0, 10)

    block = jnp.transpose(volume, (1, 2, 0, 3)).reshape(4, 16, 256)
    own = lax.all_to_all(jnp.broadcast_to(block[None], (8, 4, 16, 256)), "yz", 0, 0)
    low, high = moved(own, 1), moved(own, -1)
    field = (pltpu.VMEM((12, 160, 256), bf16), pltpu.VMEM((384, 192), bf16))
    stats = call(first_sums_kernel, statistics, "VVVV", field)(low, own, high, taps_one)
    raw = call(
        first_rows_kernel,
        shape((10, 512, 256)),
        "VVVV",
        (*field, pltpu.VMEM((10, 512, 256), f32), arrivals((10,))),
        "H",
        large,
    )(low, own, high, taps_one)

    inputs = (place, raw, swap(stats), line(offset_one), taps_two)
    field = (
        pltpu.VMEM((10, 512, 256), f32),
        arrivals((10,)),
        pltpu.VMEM((10, 544, 256), bf16),
        pltpu.VMEM((384, 480), bf16),
    )
    stats = call(bind(second_sums_kernel, count), statistics, "SHVVV", field, grant=large)(*inputs)
    raw = call(
        bind(second_rows_kernel, count),
        shape((8, 512, 256)),
        "SHVVV",
        (*field, pltpu.VMEM((8, 512, 256), f32), arrivals((8,))),
        "H",
        large,
    )(*inputs)

    raw, stats = call(
        bind(third_kernel, count),
        (shape((2, 512, 128)), statistics),
        "SHVVV",
        (
            pltpu.VMEM((8, 512, 256), f32),
            arrivals((8,)),
            pltpu.VMEM((4, 288, 128), bf16),
            pltpu.VMEM((768, 480), bf16),
        ),
        grant=large,
    )(place, raw, swap(stats), line(offset_two), tap_rows(weight_three, 0, 10))

    middle, pooled = call(
        bind(middle_kernel, count),
        (shape((2, 512, 128), bf16), shape((512, 32), bf16)),
        "VVV",
    )(raw, swap(stats), line(offset_three))
    low, high = moved(pooled, 1), moved(pooled, -1)
    taps_four = weight_four.reshape(27, 32, 128)
    raw, stats, low, high = call(
        fourth_kernel,
        (shape((512, 128)), statistics, shape((512, 32), bf16), shape((512, 32), bf16)),
        "VVVV",
    )(low, pooled, high, taps_four)
    raw, stats = call(
        bind(fifth_kernel, count),
        (shape((512, 128)), statistics),
        "SVVVVVVVVVV",
        (pltpu.VMEM((512, 1152), bf16), pltpu.VMEM((1152, 384), bf16)),
    )(
        place,
        moved(low, 1),
        low,
        pooled,
        high,
        moved(high, -1),
        raw,
        swap(stats),
        offset_four[None],
        taps_four,
        weight_five.reshape(27, 128, 128),
    )
    decoded = call(
        bind(decode_kernel, count),
        shape((128, 128), bf16),
        "SVVVVV",
    )(stripe, raw, swap(stats), offset_five[None], weight_up.T, middle)
    return decoded.reshape(32, 2, 2, 128)


def solution(mesh):
    return jax.shard_map(
        shards,
        mesh=mesh,
        in_specs=(P(None, "gx", "yz", None), P(), P(), P(), P(), P(), P(), P(), P(), P(), P(), P()),
        out_specs=P(None, "gx", "yz", None),
        check_vma=False,
    )
```

```python
import jax
import jax.numpy as jnp
from jax import lax
from jax.experimental import pallas as pl
from jax.experimental.pallas import tpu as pltpu
from jax.sharding import PartitionSpec as P

epsilon = 1e-05
f32 = jnp.float32
bf16 = jnp.bfloat16


def iota(shape, dim):
    return lax.broadcasted_iota(jnp.int32, shape, dim)


def tap_rows(kernel, before, slots):
    taps = jnp.transpose(kernel, (2, 4, 0, 1, 3)).astype(f32)
    taps = jnp.pad(taps, ((0, 0), (0, 0), (0, 0), (before, slots - 3 - before), (0, 0)))
    out, inner = kernel.shape[4], kernel.shape[3]
    taps = taps.reshape(3 * out, 3 * slots * inner)
    return jnp.pad(taps, ((0, 0), (0, -taps.shape[1] % 128)))


def fill_band(taps, band, step, out):
    depth = band.shape[1]
    base = taps[...]
    for row in range(8):
        moved = base if row == 0 else pltpu.roll(base, row * step, 1)
        for dz in range(3):
            start = (dz * 8 + row) * out
            band[start : start + out, :] = moved[dz * out : (dz + 1) * out, :depth].astype(bf16)


def merge_depth(parts, rows):
    width = parts.shape[1]
    lane = iota((rows, width), 1)
    before = jnp.where(lane == 0, 0.0, pltpu.roll(parts[:rows], 1, 1))
    after = jnp.where(lane == width - 1, 0.0, pltpu.roll(parts[2 * rows :], width - 1, 1))
    return parts[rows : 2 * rows] + before + after


def put_stats(stats, sums, squares):
    count = stats.shape[0]
    none = jnp.zeros((128 - sums.shape[0], 128), f32)
    lines = [
        jnp.sum(jnp.concatenate([part, none], axis=0).T, axis=0, keepdims=True) for part in (sums, squares)
    ]
    stats[...] = jnp.broadcast_to(jnp.concatenate(lines, axis=0)[None], (count, 2, 128))


def folded(value, channels):
    width = value.shape[1]
    total = value[:, :128]
    for start in range(128, width, 128):
        total = total + value[:, start : start + 128]
    return jnp.sum(total.reshape(-1, channels, 128), axis=0)


def row_factors(stats, offset, channels, cells):
    total = jnp.sum(stats[...], axis=0)
    lane = iota((128, 128), 1)
    same = (iota((128, 128), 0) & (channels - 1)) == (lane & (channels - 1))

    def column(line, keep):
        return jnp.sum(jnp.where(keep, line, 0.0), axis=1, keepdims=True)

    average = column(total[0:1], same) / cells
    variance = column(total[1:2], same) / cells - average * average
    shift = column(offset[...], jnp.logical_and(same, lane < channels))
    return average, lax.rsqrt(variance + epsilon), shift


def lane_factors(stats, offset, cells):
    total = jnp.sum(stats[...], axis=0)
    average = total[0:1] / cells
    variance = total[1:2] / cells - average * average
    return average, lax.rsqrt(variance + epsilon), offset[...]


def normed(value, factors):
    average, inverse, shift = factors
    return jnp.maximum((value - average) * inverse + shift, 0.0)


def put_volume(place, near, across, own, field, rows):
    def put(low, high):
        for x in rows:
            part = (low, own, high)[x // 4]
            for block in range(8):
                field[x, 16 + 16 * block : 32 + 16 * block, :] = part[block, x % 4]

    for x in rows:
        field[x, 0:16, :] = jnp.zeros((16, 256), bf16)
        field[x, 144:160, :] = jnp.zeros((16, 256), bf16)
    odd = place[0] & 1
    pl.when(odd == 0)(lambda: put(across, near))
    pl.when(odd == 1)(lambda: put(near, across))


def first_block(field, band, x, group):
    window = jnp.concatenate(
        [field[x + dx, 32 * group : 32 * group + 64, :] for dx in range(3)], axis=0
    )
    return merge_depth(jnp.dot(band[...], window, preferred_element_type=f32), 128)


def second_block(field, band, x, group):
    window = jnp.concatenate(
        [field[x + dx, 128 * group : 128 * group + 160, :] for dx in range(3)], axis=0
    )
    return merge_depth(jnp.dot(band[...], window, preferred_element_type=f32), 128)


def own_rows(block, field, band, begin, target, stats, sent=None):
    def step(x, carry):
        sums, squares = carry
        for group in range(4):
            result = block(field, band, begin + x, group)
            target[x, 128 * group : 128 * group + 128, :] = result
            sums = sums + folded(result, 16)
            squares = squares + folded(result * result, 16)
        if sent is not None:
            sent(x).start()
        return sums, squares

    none = jnp.zeros((16, 128), f32)
    sums, squares = lax.fori_loop(0, 4, step, (none, none), unroll=2)
    put_stats(stats, sums, squares)
    if sent is not None:
        for x in range(4):
            sent(x).wait()


def side_rows(block, field, band, half, gap, value, staged, left, spread=False):
    def sent(x):
        row = x + jnp.where(x < half, 0, gap)
        return pltpu.make_async_copy(staged.at[x], value.at[row if spread else x], left.at[x])

    def step(x, carry):
        row = x + jnp.where(x < half, 0, gap)
        for group in range(4):
            staged[x, 128 * group : 128 * group + 128, :] = block(field, band, row, group)
        sent(x).start()
        return carry

    lax.fori_loop(0, 2 * half, step, 0, unroll=2)
    for x in range(2 * half):
        sent(x).wait()


def bands_kernel(taps_one, taps_two, taps_three, one, two, three):
    fill_band(taps_one, one, 4, 16)
    fill_band(taps_two, two, 16, 16)
    fill_band(taps_three, three, 16, 32)


def first_own_kernel(place, near, across, own, band, value, stats, field, staged, left):
    put_volume(place, near, across, own, field, range(3, 9))

    def sent(x):
        return pltpu.make_async_copy(staged.at[x], value.at[3 + x], left.at[x])

    own_rows(first_block, field, band, 3, staged, stats, sent)


def first_side_kernel(place, near, across, own, band, value, field, staged, left):
    put_volume(place, near, across, own, field, range(12))
    side_rows(first_block, field, band, 3, 4, value, staged, left)


def put_first(count, place, own, side, raw, arrived, before, offset, field, rows):
    copies = []
    for x in rows:
        source = own.at[x] if 3 <= x < 7 else side.at[x if x < 3 else x - 4]
        copies.append(pltpu.make_async_copy(source, raw.at[x], arrived.at[x]))
        copies[-1].start()
    factors = row_factors(before, offset, 16, count * 4 * 32 * 256)
    start = place[0] * 4 - 3
    for x, copy in zip(rows, copies):
        copy.wait()
        inside = jnp.logical_and(start + x >= 0, start + x < count * 4)
        field[x, 0:16, :] = jnp.zeros((16, 256), bf16)
        field[x, 528:544, :] = jnp.zeros((16, 256), bf16)
        for group in range(4):
            active = normed(raw[x, 128 * group : 128 * group + 128, :], factors)
            active = jnp.where(inside, active, 0.0).astype(bf16)
            field[x, 16 + 128 * group : 144 + 128 * group, :] = active


def second_own_kernel(
    count, place, own, side, before, offset, band, value, stats, raw, arrived, field
):
    put_first(count, place, own, side, raw, arrived, before, offset, field, range(2, 8))
    own_rows(second_block, field, band, 2, value, stats)


def second_side_kernel(
    count, place, own, side, before, offset, band, value, raw, arrived, field, staged, left
):
    put_first(count, place, own, side, raw, arrived, before, offset, field, (0, 1, 2, 3, 6, 7, 8, 9))
    side_rows(second_block, field, band, 2, 4, value, staged, left, spread=True)


def third_kernel(
    count, place, own, side, before, offset, band, value, stats, raw, arrived, field
):
    copies = {x: pltpu.make_async_copy(side.at[x], raw.at[x], arrived.at[x]) for x in (0, 1, 6, 7)}
    for copy in copies.values():
        copy.start()
    factors = row_factors(before, offset, 16, count * 4 * 32 * 256)
    halve = jnp.where((iota((256, 128), 0) >> 1) == iota((256, 128), 1), 0.125, 0.0).astype(bf16)
    start = place[0] * 2 - 1
    for x in (1, 2, 0, 3):
        if 2 * x in copies:
            copies[2 * x].wait()
            copies[2 * x + 1].wait()
        inside = jnp.logical_and(start + x >= 0, start + x < count * 2)
        field[x, 0:16, :] = jnp.zeros((16, 128), bf16)
        field[x, 272:288, :] = jnp.zeros((16, 128), bf16)
        for group in range(4):
            total = None
            for half in range(2):
                row = 2 * x + half
                source = raw.at[row] if row in copies else own.at[row - 2]
                active = normed(source[128 * group : 128 * group + 128, :], factors)
                part = jnp.dot(active.astype(bf16), halve, preferred_element_type=f32)
                total = part if total is None else total + part
            total = jnp.sum(total.reshape(4, 2, 16, 128), axis=1).reshape(64, 128)
            total = jnp.where(inside, total, 0.0).astype(bf16)
            field[x, 16 + 64 * group : 80 + 64 * group, :] = total
    sums = jnp.zeros((32, 128), f32)
    squares = jnp.zeros((32, 128), f32)
    for x in range(2):
        window = jnp.concatenate(
            [
                jnp.concatenate([field[x + dx, 128 * group : 128 * group + 160, :] for dx in range(3)], axis=0)
                for group in range(2)
            ],
            axis=1,
        )
        parts = jnp.dot(band[...], window, preferred_element_type=f32)
        for group in range(2):
            result = merge_depth(parts[:, 128 * group : 128 * group + 128], 256)
            value[x, 256 * group : 256 * group + 256, :] = result
            sums = sums + folded(result, 32)
            squares = squares + folded(result * result, 32)
    put_stats(stats, sums, squares)


def middle_kernel(count, raw, before, offset, middle, pooled):
    factors = row_factors(before, offset, 32, count * 2 * 16 * 128)
    for x in range(2):
        for group in range(4):
            active = normed(raw[x, 128 * group : 128 * group + 128, :], factors).astype(bf16)
            middle[x, 128 * group : 128 * group + 128, :] = active
    halve = jnp.where(((iota((64, 512), 1) & 127) >> 1) == iota((64, 512), 0), 0.125, 0.0).astype(bf16)
    for part in range(2):
        cells = jnp.concatenate(
            [
                jnp.concatenate(
                    [middle[x, 64 * y + 32 * side : 64 * y + 32 * side + 32, :] for y in range(4 * part, 4 * part + 4)],
                    axis=0,
                )
                for x in range(2)
                for side in range(2)
            ],
            axis=1,
        )
        total = lax.dot_general(halve, cells, (((1,), (1,)), ((), ())), preferred_element_type=f32)
        pooled[64 * part : 64 * part + 64, :] = total.astype(bf16)


def unpacked(pooled):
    pooled = pooled.astype(f32)
    return jnp.concatenate(
        [
            pooled[64 * part : 64 * part + 64, 32 * side : 32 * side + 32]
            for part in range(2)
            for side in range(4)
        ],
        axis=0,
    )


def along_depth(value):
    rows = value.shape[0]
    depth = iota(value.shape, 0) & 63
    before = jnp.where(depth == 0, 0.0, pltpu.roll(value, 1, 0))
    after = jnp.where(depth == 63, 0.0, pltpu.roll(value, rows - 1, 0))
    return before, value, after


def merge_side(parts):
    none = jnp.zeros((64, 128), f32)
    return (
        parts[:, 128:256]
        + jnp.concatenate([none, parts[:-64, 0:128]], axis=0)
        + jnp.concatenate([parts[64:, 256:384], none], axis=0)
    )


def put_lane_stats(stats, result):
    count = stats.shape[0]
    line = jnp.concatenate(
        [jnp.sum(result, axis=0, keepdims=True), jnp.sum(result * result, axis=0, keepdims=True)], axis=0
    )
    stats[...] = jnp.broadcast_to(line[None], (count, 2, 128))


def fourth_row(parts, kernel):
    taps = jnp.concatenate(
        [
            jnp.concatenate([kernel[dx * 9 + dy * 3 + dz] for dy in range(3)], axis=1)
            for dx in range(3)
            for dz in range(3)
        ],
        axis=0,
    )
    window = jnp.concatenate(
        [view.astype(bf16) for part in parts for view in along_depth(part)], axis=1
    )
    return merge_side(jnp.dot(window, taps, preferred_element_type=f32))


def in_order(place, near, across):
    odd = (place[0] & 1) == 1
    return jnp.where(odd, near, across), jnp.where(odd, across, near)


def fourth_kernel(place, near, across, own, kernel, value, stats, passed):
    low, high = in_order(place, unpacked(near[...]), unpacked(across[0]))
    result = fourth_row((low, unpacked(own[...]), high), kernel)
    value[...] = result
    put_lane_stats(stats, result)
    passed[...] = across[0]


def fifth_kernel(
    count, place, near, across, passed, own, raw, before, offset, kernel_four, kernel, value, stats, field, taps
):
    centre = unpacked(own[...])
    low, high = in_order(place, unpacked(near[...]), unpacked(across[0]))
    far_low, far_high = in_order(place, unpacked(passed[...]), unpacked(across[1]))
    parts = (
        fourth_row((far_low, low, centre), kernel_four),
        raw[...],
        fourth_row((centre, high, far_high), kernel_four),
    )
    factors = lane_factors(before, offset, count * 8 * 64)
    for dx in range(3):
        for dz in range(3):
            row = (dx * 3 + dz) * 128
            for dy in range(3):
                taps[row : row + 128, dy * 128 : dy * 128 + 128] = kernel[dx * 9 + dy * 3 + dz]
    start = place[0] - 1
    for x, part in enumerate(parts):
        inside = jnp.logical_and(start + x >= 0, start + x < count)
        active = jnp.where(inside, normed(part, factors), 0.0)
        for dz, view in enumerate(along_depth(active)):
            lane = (x * 3 + dz) * 128
            field[:, lane : lane + 128] = view.astype(bf16)
    parts = jnp.dot(field[...], taps[...], preferred_element_type=f32)
    result = merge_side(parts)
    value[...] = result
    put_lane_stats(stats, result)


def decode_kernel(count, place, raw, before, offset, up, middle, decoded):
    factors = lane_factors(before, offset, count * 8 * 64)
    stripe = place[0]
    active = normed(raw[pl.ds(pl.multiple_of(stripe * 64, 64), 64), :], factors).astype(bf16)
    twice = jnp.where((iota((128, 64), 0) >> 1) == iota((128, 64), 1), 1.0, 0.0).astype(bf16)
    active = jnp.dot(twice, active, preferred_element_type=f32).astype(bf16)
    projected = lax.dot_general(up[...], active, (((1,), (1,)), ((), ())), preferred_element_type=f32)
    blocks = []
    for x in range(2):
        own = middle[x, pl.ds(pl.multiple_of(stripe * 64, 64), 64), :].astype(f32)
        for side in range(2):
            merged = jnp.maximum(projected + own[32 * side : 32 * side + 32], 0.0)
            blocks.append(merged.astype(bf16))
    blocks = jnp.concatenate(blocks, axis=0)
    row = iota((128, 128), 0)
    order = jnp.where(((row & 3) * 32 + (row >> 2)) == iota((128, 128), 1), 1.0, 0.0).astype(bf16)
    decoded[...] = jnp.dot(order, blocks, preferred_element_type=f32).astype(bf16)


def shape(dims, kind=f32):
    return jax.ShapeDtypeStruct(dims, kind)


def call(kernel, outs, places, scratch=(), out_places=None, grant=28):
    spaces = {"S": pltpu.SMEM, "V": pltpu.VMEM, "H": pltpu.HBM}

    def specs(letters):
        return tuple(pl.BlockSpec(memory_space=spaces[letter]) for letter in letters)

    single = not isinstance(outs, tuple)
    out_specs = specs(out_places or "V" * (1 if single else len(outs)))
    return pl.pallas_call(
        kernel,
        out_shape=outs,
        in_specs=specs(places),
        out_specs=out_specs[0] if single else out_specs,
        scratch_shapes=list(scratch),
        compiler_params=pltpu.CompilerParams(vmem_limit_bytes=grant * 1024 * 1024),
        cost_estimate=pl.CostEstimate(flops=1 << 30, bytes_accessed=1 << 22, transcendentals=0),
    )


def swap(stats):
    return lax.all_to_all(stats, "gx", 0, 0)


def bind(kernel, count):
    def bound(*refs):
        kernel(count, *refs)

    return bound


def shards(
    volume,
    weight_one,
    offset_one,
    weight_two,
    offset_two,
    weight_three,
    offset_three,
    weight_four,
    offset_four,
    weight_five,
    offset_five,
    weight_up,
):
    count = lax.axis_size("gx")
    place = lax.axis_index("gx").astype(jnp.int32)[None]
    stripe = lax.axis_index("yz").astype(jnp.int32)[None]

    def swapped(block, first):
        pairs = [(i, i + 1) for i in range(first, count - 1, 2)]
        return lax.ppermute(block, "gx", pairs + [(target, source) for source, target in pairs])

    def line(offset):
        return jnp.pad(offset, (0, 128 - offset.shape[0]))[None]

    statistics = shape((count, 2, 128))
    large, medium, small = 51, 51, 48
    arrivals = pltpu.SemaphoreType.DMA
    band_one, band_two, band_three = call(
        bands_kernel,
        (shape((384, 192), bf16), shape((384, 480), bf16), shape((768, 480), bf16)),
        "VVV",
    )(tap_rows(weight_one, 3, 16), tap_rows(weight_two, 0, 10), tap_rows(weight_three, 0, 10))

    block = jnp.transpose(volume, (1, 2, 0, 3)).reshape(4, 16, 256)
    own = lax.all_to_all(jnp.broadcast_to(block[None], (8, 4, 16, 256)), "yz", 0, 0)
    across, near = swapped(own, 1), swapped(own, 0)

    def staged(rows):
        return (pltpu.VMEM((rows, 512, 256), f32), arrivals((rows,)))

    inputs = (place, near, across, own, band_one)
    field = (pltpu.VMEM((12, 160, 256), bf16),)
    raw, stats = call(
        first_own_kernel,
        (shape((10, 512, 256)), statistics),
        "SVVVV",
        (*field, *staged(4)),
        "HV",
        large,
    )(*inputs)
    side = call(first_side_kernel, shape((6, 512, 256)), "SVVVV", (*field, *staged(6)), "H", large)(*inputs)

    inputs = (place, raw, side, swap(stats), line(offset_one), band_two)
    field = (*staged(10), pltpu.VMEM((10, 544, 256), bf16))
    raw, stats = call(
        bind(second_own_kernel, count),
        (shape((4, 512, 256)), statistics),
        "SHHVVV",
        field,
        grant=large,
    )(*inputs)
    side = call(
        bind(second_side_kernel, count),
        shape((8, 512, 256)),
        "SHHVVV",
        (*field, *staged(4)),
        "H",
        medium,
    )(*inputs)

    raw, stats = call(
        bind(third_kernel, count),
        (shape((2, 512, 128)), statistics),
        "SVHVVV",
        (*staged(8), pltpu.VMEM((4, 288, 128), bf16)),
        grant=small,
    )(place, raw, side, swap(stats), line(offset_two), band_three)

    middle, pooled = call(
        bind(middle_kernel, count),
        (shape((2, 512, 128), bf16), shape((128, 128), bf16)),
        "VVV",
    )(raw, swap(stats), line(offset_three))
    near = swapped(pooled, 0)
    across = swapped(jnp.stack([pooled, near]), 1)
    taps_four = weight_four.reshape(27, 32, 128)
    raw, stats, passed = call(
        fourth_kernel,
        (shape((512, 128)), statistics, shape((128, 128), bf16)),
        "SVVVV",
    )(place, near, across, pooled, taps_four)
    raw, stats = call(
        bind(fifth_kernel, count),
        (shape((512, 128)), statistics),
        "SVVVVVVVVV",
        (pltpu.VMEM((512, 1152), bf16), pltpu.VMEM((1152, 384), bf16)),
    )(
        place,
        near,
        across,
        swapped(passed, 0),
        pooled,
        raw,
        swap(stats),
        offset_four[None],
        taps_four,
        weight_five.reshape(27, 128, 128),
    )
    decoded = call(
        bind(decode_kernel, count),
        shape((128, 128), bf16),
        "SVVVVV",
    )(stripe, raw, swap(stats), offset_five[None], weight_up.T, middle)
    return decoded.reshape(32, 2, 2, 128)


def solution(mesh):
    return jax.shard_map(
        shards,
        mesh=mesh,
        in_specs=(P(None, "gx", "yz", None), P(), P(), P(), P(), P(), P(), P(), P(), P(), P(), P()),
        out_specs=P(None, "gx", "yz", None),
        check_vma=False,
    )
```

```python
import jax
import jax.numpy as jnp
from jax import lax
from jax.experimental import pallas as pl
from jax.experimental.pallas import tpu as pltpu
from jax.sharding import PartitionSpec as P

epsilon = 1e-05
f32 = jnp.float32
bf16 = jnp.bfloat16


def iota(shape, dim):
    return lax.broadcasted_iota(jnp.int32, shape, dim)


def tap_rows(kernel, before, slots):
    taps = jnp.transpose(kernel, (2, 4, 0, 1, 3)).astype(f32)
    taps = jnp.pad(taps, ((0, 0), (0, 0), (0, 0), (before, slots - 3 - before), (0, 0)))
    out, inner = kernel.shape[4], kernel.shape[3]
    taps = taps.reshape(3 * out, 3 * slots * inner)
    return jnp.pad(taps, ((0, 0), (0, -taps.shape[1] % 128)))


def fill_band(taps, band, step, out):
    depth = band.shape[1]
    base = taps[...]
    for row in range(8):
        moved = base if row == 0 else pltpu.roll(base, row * step, 1)
        for dz in range(3):
            start = (dz * 8 + row) * out
            band[start : start + out, :] = moved[dz * out : (dz + 1) * out, :depth].astype(bf16)


def merge_depth(parts, rows):
    width = parts.shape[1]
    lane = iota((rows, width), 1)
    before = jnp.where(lane == 0, 0.0, pltpu.roll(parts[:rows], 1, 1))
    after = jnp.where(lane == width - 1, 0.0, pltpu.roll(parts[2 * rows :], width - 1, 1))
    return parts[rows : 2 * rows] + before + after


def put_stats(stats, sums, squares):
    count = stats.shape[0]
    none = jnp.zeros((128 - sums.shape[0], 128), f32)
    lines = [
        jnp.sum(jnp.concatenate([part, none], axis=0).T, axis=0, keepdims=True) for part in (sums, squares)
    ]
    stats[...] = jnp.broadcast_to(jnp.concatenate(lines, axis=0)[None], (count, 2, 128))


def folded(value, channels):
    width = value.shape[1]
    total = value[:, :128]
    for start in range(128, width, 128):
        total = total + value[:, start : start + 128]
    return jnp.sum(total.reshape(-1, channels, 128), axis=0)


def row_factors(stats, offset, channels, cells):
    total = jnp.sum(stats[...], axis=0)
    lane = iota((128, 128), 1)
    same = (iota((128, 128), 0) & (channels - 1)) == (lane & (channels - 1))

    def column(line, keep):
        return jnp.sum(jnp.where(keep, line, 0.0), axis=1, keepdims=True)

    average = column(total[0:1], same) / cells
    variance = column(total[1:2], same) / cells - average * average
    shift = column(offset[...], jnp.logical_and(same, lane < channels))
    return average, lax.rsqrt(variance + epsilon), shift


def lane_factors(stats, offset, cells):
    total = jnp.sum(stats[...], axis=0)
    average = total[0:1] / cells
    variance = total[1:2] / cells - average * average
    return average, lax.rsqrt(variance + epsilon), offset[...]


def normed(value, factors):
    average, inverse, shift = factors
    return jnp.maximum((value - average) * inverse + shift, 0.0)


def put_volume(place, near, across, own, field, rows):
    def put(low, high):
        for x in rows:
            part = (low, own, high)[x // 4]
            for block in range(8):
                field[x, 16 + 16 * block : 32 + 16 * block, :] = part[block, x % 4]

    for x in rows:
        field[x, 0:16, :] = jnp.zeros((16, 256), bf16)
        field[x, 144:160, :] = jnp.zeros((16, 256), bf16)
    odd = place[0] & 1
    pl.when(odd == 0)(lambda: put(across, near))
    pl.when(odd == 1)(lambda: put(near, across))


def first_block(field, band, x, group):
    window = jnp.concatenate(
        [field[x + dx, 32 * group : 32 * group + 64, :] for dx in range(3)], axis=0
    )
    return merge_depth(jnp.dot(band[...], window, preferred_element_type=f32), 128)


def second_block(field, band, x, group):
    window = jnp.concatenate(
        [field[x + dx, 128 * group : 128 * group + 160, :] for dx in range(3)], axis=0
    )
    return merge_depth(jnp.dot(band[...], window, preferred_element_type=f32), 128)


def own_rows(block, field, band, begin, stats, value=None):
    def step(x, carry):
        sums, squares = carry
        for group in range(4):
            result = block(field, band, begin + x, group)
            if value is not None:
                value[x, 128 * group : 128 * group + 128, :] = result
            sums = sums + folded(result, 16)
            squares = squares + folded(result * result, 16)
        return sums, squares

    none = jnp.zeros((16, 128), f32)
    sums, squares = lax.fori_loop(0, 4, step, (none, none), unroll=2)
    put_stats(stats, sums, squares)


def side_rows(block, field, band, rows, gap, value, staged, left):
    def sent(x):
        row = x + jnp.where(x < rows // 2, 0, gap)
        return pltpu.make_async_copy(staged.at[x], value.at[row], left.at[x])

    def step(x, carry):
        row = x + jnp.where(x < rows // 2, 0, gap)
        for group in range(4):
            staged[x, 128 * group : 128 * group + 128, :] = block(field, band, row, group)
        sent(x).start()
        return carry

    lax.fori_loop(0, rows, step, 0, unroll=2)
    for x in range(rows):
        sent(x).wait()


def bands_kernel(taps_one, taps_two, taps_three, one, two, three):
    fill_band(taps_one, one, 4, 16)
    fill_band(taps_two, two, 16, 16)
    fill_band(taps_three, three, 16, 32)


def first_sums_kernel(place, near, across, own, band, stats, field):
    put_volume(place, near, across, own, field, range(3, 9))
    own_rows(first_block, field, band, 3, stats)


def first_rows_kernel(place, near, across, own, band, value, field, staged, left):
    put_volume(place, near, across, own, field, range(12))
    side_rows(first_block, field, band, 10, 0, value, staged, left)


def put_first(count, place, source, raw, arrived, before, offset, field, rows):
    copies = [pltpu.make_async_copy(source.at[x], raw.at[x], arrived.at[x]) for x in rows]
    for copy in copies:
        copy.start()
    factors = row_factors(before, offset, 16, count * 4 * 32 * 256)
    start = place[0] * 4 - 3
    for x, copy in zip(rows, copies):
        copy.wait()
        inside = jnp.logical_and(start + x >= 0, start + x < count * 4)
        field[x, 0:16, :] = jnp.zeros((16, 256), bf16)
        field[x, 528:544, :] = jnp.zeros((16, 256), bf16)
        for group in range(4):
            active = normed(raw[x, 128 * group : 128 * group + 128, :], factors)
            active = jnp.where(inside, active, 0.0).astype(bf16)
            field[x, 16 + 128 * group : 144 + 128 * group, :] = active


def second_own_kernel(
    count, place, source, before, offset, band, value, stats, raw, arrived, field
):
    put_first(count, place, source, raw, arrived, before, offset, field, range(2, 8))
    own_rows(second_block, field, band, 2, stats, value)


def second_side_kernel(
    count, place, source, before, offset, band, value, raw, arrived, field, staged, left
):
    put_first(count, place, source, raw, arrived, before, offset, field, (0, 1, 2, 3, 6, 7, 8, 9))
    side_rows(second_block, field, band, 4, 4, value, staged, left)


def third_kernel(
    count, place, own, side, before, offset, band, value, stats, raw, arrived, field
):
    copies = {x: pltpu.make_async_copy(side.at[x], raw.at[x], arrived.at[x]) for x in (0, 1, 6, 7)}
    for copy in copies.values():
        copy.start()
    factors = row_factors(before, offset, 16, count * 4 * 32 * 256)
    halve = jnp.where((iota((256, 128), 0) >> 1) == iota((256, 128), 1), 0.125, 0.0).astype(bf16)
    start = place[0] * 2 - 1
    for x in (1, 2, 0, 3):
        if 2 * x in copies:
            copies[2 * x].wait()
            copies[2 * x + 1].wait()
        inside = jnp.logical_and(start + x >= 0, start + x < count * 2)
        field[x, 0:16, :] = jnp.zeros((16, 128), bf16)
        field[x, 272:288, :] = jnp.zeros((16, 128), bf16)
        for group in range(4):
            total = None
            for half in range(2):
                row = 2 * x + half
                source = raw.at[row] if row in copies else own.at[row - 2]
                active = normed(source[128 * group : 128 * group + 128, :], factors)
                part = jnp.dot(active.astype(bf16), halve, preferred_element_type=f32)
                total = part if total is None else total + part
            total = jnp.sum(total.reshape(4, 2, 16, 128), axis=1).reshape(64, 128)
            total = jnp.where(inside, total, 0.0).astype(bf16)
            field[x, 16 + 64 * group : 80 + 64 * group, :] = total
    sums = jnp.zeros((32, 128), f32)
    squares = jnp.zeros((32, 128), f32)
    for x in range(2):
        window = jnp.concatenate(
            [
                jnp.concatenate([field[x + dx, 128 * group : 128 * group + 160, :] for dx in range(3)], axis=0)
                for group in range(2)
            ],
            axis=1,
        )
        parts = jnp.dot(band[...], window, preferred_element_type=f32)
        for group in range(2):
            result = merge_depth(parts[:, 128 * group : 128 * group + 128], 256)
            value[x, 256 * group : 256 * group + 256, :] = result
            sums = sums + folded(result, 32)
            squares = squares + folded(result * result, 32)
    put_stats(stats, sums, squares)


def middle_kernel(count, raw, near, before, offset, middle, pooled, partner):
    factors = row_factors(before, offset, 32, count * 2 * 16 * 128)
    halve = jnp.where(((iota((64, 512), 1) & 127) >> 1) == iota((64, 512), 0), 0.125, 0.0).astype(bf16)
    for place, (source, target) in enumerate(((raw, middle), (near, partner))):
        for x in range(2):
            for group in range(4):
                active = normed(source[x, 128 * group : 128 * group + 128, :], factors).astype(bf16)
                target[x, 128 * group : 128 * group + 128, :] = active
        for part in range(2):
            cells = jnp.concatenate(
                [
                    jnp.concatenate(
                        [
                            target[x, 64 * y + 32 * side : 64 * y + 32 * side + 32, :]
                            for y in range(4 * part, 4 * part + 4)
                        ],
                        axis=0,
                    )
                    for x in range(2)
                    for side in range(2)
                ],
                axis=1,
            )
            total = lax.dot_general(halve, cells, (((1,), (1,)), ((), ())), preferred_element_type=f32)
            pooled[place, 64 * part : 64 * part + 64, :] = total.astype(bf16)


def unpacked(pooled):
    pooled = pooled.astype(f32)
    return jnp.concatenate(
        [
            pooled[64 * part : 64 * part + 64, 32 * side : 32 * side + 32]
            for part in range(2)
            for side in range(4)
        ],
        axis=0,
    )


def along_depth(value):
    rows = value.shape[0]
    depth = iota(value.shape, 0) & 63
    before = jnp.where(depth == 0, 0.0, pltpu.roll(value, 1, 0))
    after = jnp.where(depth == 63, 0.0, pltpu.roll(value, rows - 1, 0))
    return before, value, after


def merge_side(parts):
    none = jnp.zeros((64, 128), f32)
    return (
        parts[:, 128:256]
        + jnp.concatenate([none, parts[:-64, 0:128]], axis=0)
        + jnp.concatenate([parts[64:, 256:384], none], axis=0)
    )


def put_lane_stats(stats, result):
    count = stats.shape[0]
    line = jnp.concatenate(
        [jnp.sum(result, axis=0, keepdims=True), jnp.sum(result * result, axis=0, keepdims=True)], axis=0
    )
    stats[...] = jnp.broadcast_to(line[None], (count, 2, 128))


def fourth_row(parts, kernel):
    taps = jnp.concatenate(
        [
            jnp.concatenate([kernel[dx * 9 + dy * 3 + dz] for dy in range(3)], axis=1)
            for dx in range(3)
            for dz in range(3)
        ],
        axis=0,
    )
    window = jnp.concatenate(
        [view.astype(bf16) for part in parts for view in along_depth(part)], axis=1
    )
    return merge_side(jnp.dot(window, taps, preferred_element_type=f32))


def in_order(place, near, across):
    odd = (place[0] & 1) == 1
    return jnp.where(odd, near, across), jnp.where(odd, across, near)


def fourth_kernel(place, pooled, across, kernel, value, stats, passed):
    low, high = in_order(place, unpacked(pooled[1]), unpacked(across[0]))
    result = fourth_row((low, unpacked(pooled[0]), high), kernel)
    value[...] = result
    put_lane_stats(stats, result)
    passed[...] = across[0]


def fifth_kernel(
    count, place, pooled, across, passed, raw, before, offset, kernel_four, kernel, value, stats, field, taps
):
    centre = unpacked(pooled[0])
    low, high = in_order(place, unpacked(pooled[1]), unpacked(across[0]))
    far_low, far_high = in_order(place, unpacked(passed[...]), unpacked(across[1]))
    parts = (
        fourth_row((far_low, low, centre), kernel_four),
        raw[...],
        fourth_row((centre, high, far_high), kernel_four),
    )
    factors = lane_factors(before, offset, count * 8 * 64)
    for dx in range(3):
        for dz in range(3):
            row = (dx * 3 + dz) * 128
            for dy in range(3):
                taps[row : row + 128, dy * 128 : dy * 128 + 128] = kernel[dx * 9 + dy * 3 + dz]
    start = place[0] - 1
    for x, part in enumerate(parts):
        inside = jnp.logical_and(start + x >= 0, start + x < count)
        active = jnp.where(inside, normed(part, factors), 0.0)
        for dz, view in enumerate(along_depth(active)):
            lane = (x * 3 + dz) * 128
            field[:, lane : lane + 128] = view.astype(bf16)
    parts = jnp.dot(field[...], taps[...], preferred_element_type=f32)
    result = merge_side(parts)
    value[...] = result
    put_lane_stats(stats, result)


def decode_kernel(count, place, raw, before, offset, up, middle, decoded):
    factors = lane_factors(before, offset, count * 8 * 64)
    stripe = place[0]
    active = normed(raw[pl.ds(pl.multiple_of(stripe * 64, 64), 64), :], factors).astype(bf16)
    twice = jnp.where((iota((128, 64), 0) >> 1) == iota((128, 64), 1), 1.0, 0.0).astype(bf16)
    active = jnp.dot(twice, active, preferred_element_type=f32).astype(bf16)
    projected = lax.dot_general(up[...], active, (((1,), (1,)), ((), ())), preferred_element_type=f32)
    blocks = []
    for x in range(2):
        own = middle[x, pl.ds(pl.multiple_of(stripe * 64, 64), 64), :].astype(f32)
        for side in range(2):
            merged = jnp.maximum(projected + own[32 * side : 32 * side + 32], 0.0)
            blocks.append(merged.astype(bf16))
    blocks = jnp.concatenate(blocks, axis=0)
    row = iota((128, 128), 0)
    order = jnp.where(((row & 3) * 32 + (row >> 2)) == iota((128, 128), 1), 1.0, 0.0).astype(bf16)
    decoded[...] = jnp.dot(order, blocks, preferred_element_type=f32).astype(bf16)


def shape(dims, kind=f32):
    return jax.ShapeDtypeStruct(dims, kind)


def call(kernel, outs, places, scratch=(), out_places=None, grant=28):
    spaces = {"S": pltpu.SMEM, "V": pltpu.VMEM, "H": pltpu.HBM}

    def specs(letters):
        return tuple(pl.BlockSpec(memory_space=spaces[letter]) for letter in letters)

    single = not isinstance(outs, tuple)
    out_specs = specs(out_places or "V" * (1 if single else len(outs)))
    return pl.pallas_call(
        kernel,
        out_shape=outs,
        in_specs=specs(places),
        out_specs=out_specs[0] if single else out_specs,
        scratch_shapes=list(scratch),
        compiler_params=pltpu.CompilerParams(vmem_limit_bytes=grant * 1024 * 1024),
        cost_estimate=pl.CostEstimate(flops=1 << 30, bytes_accessed=1 << 22, transcendentals=0),
    )


def swap(stats):
    return lax.all_to_all(stats, "gx", 0, 0)


def bind(kernel, count):
    def bound(*refs):
        kernel(count, *refs)

    return bound


def shards(
    volume,
    weight_one,
    offset_one,
    weight_two,
    offset_two,
    weight_three,
    offset_three,
    weight_four,
    offset_four,
    weight_five,
    offset_five,
    weight_up,
):
    count = lax.axis_size("gx")
    place = lax.axis_index("gx").astype(jnp.int32)[None]
    stripe = lax.axis_index("yz").astype(jnp.int32)[None]

    def swapped(block, first):
        pairs = [(i, i + 1) for i in range(first, count - 1, 2)]
        return lax.ppermute(block, "gx", pairs + [(target, source) for source, target in pairs])

    def line(offset):
        return jnp.pad(offset, (0, 128 - offset.shape[0]))[None]

    statistics = shape((count, 2, 128))
    large, medium, small = 51, 51, 48
    arrivals = pltpu.SemaphoreType.DMA
    band_one, band_two, band_three = call(
        bands_kernel,
        (shape((384, 192), bf16), shape((384, 480), bf16), shape((768, 480), bf16)),
        "VVV",
    )(tap_rows(weight_one, 3, 16), tap_rows(weight_two, 0, 10), tap_rows(weight_three, 0, 10))

    block = jnp.transpose(volume, (1, 2, 0, 3)).reshape(4, 16, 256)
    own = lax.all_to_all(jnp.broadcast_to(block[None], (8, 4, 16, 256)), "yz", 0, 0)
    across, near = swapped(own, 1), swapped(own, 0)

    def staged(rows):
        return (pltpu.VMEM((rows, 512, 256), f32), arrivals((rows,)))

    inputs = (place, near, across, own, band_one)
    field = (pltpu.VMEM((12, 160, 256), bf16),)
    stats = call(first_sums_kernel, statistics, "SVVVV", field, grant=large)(*inputs)
    rows = call(
        first_rows_kernel, shape((10, 512, 256)), "SVVVV", (*field, *staged(10)), "H", large
    )(*inputs)

    inputs = (place, rows, swap(stats), line(offset_one), band_two)
    field = (*staged(10), pltpu.VMEM((10, 544, 256), bf16))
    raw, stats = call(
        bind(second_own_kernel, count),
        (shape((4, 512, 256)), statistics),
        "SHVVV",
        field,
        grant=large,
    )(*inputs)
    side = call(
        bind(second_side_kernel, count),
        shape((8, 512, 256)),
        "SHVVV",
        (*field, *staged(4)),
        "H",
        medium,
    )(*inputs)

    raw, stats = call(
        bind(third_kernel, count),
        (shape((2, 512, 128)), statistics),
        "SVHVVV",
        (*staged(8), pltpu.VMEM((4, 288, 128), bf16)),
        grant=small,
    )(place, raw, side, swap(stats), line(offset_two), band_three)

    middle, pooled = call(
        bind(middle_kernel, count),
        (shape((2, 512, 128), bf16), shape((2, 128, 128), bf16)),
        "VVVV",
        (pltpu.VMEM((2, 512, 128), bf16),),
    )(raw, swapped(raw, 0), swap(stats), line(offset_three))
    across = swapped(pooled, 1)
    taps_four = weight_four.reshape(27, 32, 128)
    raw, stats, passed = call(
        fourth_kernel,
        (shape((512, 128)), statistics, shape((128, 128), bf16)),
        "SVVV",
    )(place, pooled, across, taps_four)
    raw, stats = call(
        bind(fifth_kernel, count),
        (shape((512, 128)), statistics),
        "SVVVVVVVV",
        (pltpu.VMEM((512, 1152), bf16), pltpu.VMEM((1152, 384), bf16)),
    )(
        place,
        pooled,
        across,
        swapped(passed, 0),
        raw,
        swap(stats),
        offset_four[None],
        taps_four,
        weight_five.reshape(27, 128, 128),
    )
    decoded = call(
        bind(decode_kernel, count),
        shape((128, 128), bf16),
        "SVVVVV",
    )(stripe, raw, swap(stats), offset_five[None], weight_up.T, middle)
    return decoded.reshape(32, 2, 2, 128)


def solution(mesh):
    return jax.shard_map(
        shards,
        mesh=mesh,
        in_specs=(P(None, "gx", "yz", None), P(), P(), P(), P(), P(), P(), P(), P(), P(), P(), P()),
        out_specs=P(None, "gx", "yz", None),
        check_vma=False,
    )
```

```python
import jax
import jax.numpy as jnp
from jax import lax
from jax.experimental import pallas as pl
from jax.experimental.pallas import tpu as pltpu
from jax.sharding import PartitionSpec as P

epsilon = 1e-05
f32 = jnp.float32
bf16 = jnp.bfloat16


def iota(shape, dim):
    return lax.broadcasted_iota(jnp.int32, shape, dim)


def tap_rows(kernel, before, slots):
    taps = jnp.transpose(kernel, (2, 4, 0, 1, 3)).astype(f32)
    taps = jnp.pad(taps, ((0, 0), (0, 0), (0, 0), (before, slots - 3 - before), (0, 0)))
    out, inner = kernel.shape[4], kernel.shape[3]
    taps = taps.reshape(3 * out, 3 * slots * inner)
    return jnp.pad(taps, ((0, 0), (0, -taps.shape[1] % 128)))


def fill_band(taps, band, step, out):
    depth = band.shape[1]
    base = taps[...]
    for row in range(8):
        moved = base if row == 0 else pltpu.roll(base, row * step, 1)
        for dz in range(3):
            start = (dz * 8 + row) * out
            band[start : start + out, :] = moved[dz * out : (dz + 1) * out, :depth].astype(bf16)


def merge_depth(parts, rows):
    width = parts.shape[1]
    lane = iota((rows, width), 1)
    before = jnp.where(lane == 0, 0.0, pltpu.roll(parts[:rows], 1, 1))
    after = jnp.where(lane == width - 1, 0.0, pltpu.roll(parts[2 * rows :], width - 1, 1))
    return parts[rows : 2 * rows] + before + after


def put_stats(stats, sums, squares):
    count = stats.shape[0]
    none = jnp.zeros((128 - sums.shape[0], 128), f32)
    lines = [
        jnp.sum(jnp.concatenate([part, none], axis=0).T, axis=0, keepdims=True) for part in (sums, squares)
    ]
    stats[...] = jnp.broadcast_to(jnp.concatenate(lines, axis=0)[None], (count, 2, 128))


def folded(value, channels):
    width = value.shape[1]
    total = value[:, :128]
    for start in range(128, width, 128):
        total = total + value[:, start : start + 128]
    return jnp.sum(total.reshape(-1, channels, 128), axis=0)


def row_factors(stats, offset, channels, cells):
    total = jnp.sum(stats[...], axis=0)
    lane = iota((128, 128), 1)
    same = (iota((128, 128), 0) & (channels - 1)) == (lane & (channels - 1))

    def column(line, keep):
        return jnp.sum(jnp.where(keep, line, 0.0), axis=1, keepdims=True)

    average = column(total[0:1], same) / cells
    variance = column(total[1:2], same) / cells - average * average
    shift = column(offset[...], jnp.logical_and(same, lane < channels))
    return average, lax.rsqrt(variance + epsilon), shift


def lane_factors(stats, offset, cells):
    total = jnp.sum(stats[...], axis=0)
    average = total[0:1] / cells
    variance = total[1:2] / cells - average * average
    return average, lax.rsqrt(variance + epsilon), offset[...]


def normed(value, factors):
    average, inverse, shift = factors
    return jnp.maximum((value - average) * inverse + shift, 0.0)


def put_volume(part, rows, field, begin):
    for x in rows:
        field[begin + x, 0:16, :] = jnp.zeros((16, 256), bf16)
        field[begin + x, 144:160, :] = jnp.zeros((16, 256), bf16)
        for block in range(8):
            field[begin + x, 16 + 16 * block : 32 + 16 * block, :] = part[block, x]


def put_sides(place, near, across, rows, field):
    odd = place[0] & 1

    def put(low, high):
        if low is not None:
            put_volume(low, range(4 - rows, 4), field, 0)
        if high is not None:
            put_volume(high, range(rows), field, 8)

    pl.when(odd == 0)(lambda: put(across, near))
    pl.when(odd == 1)(lambda: put(near, across))


def first_block(field, band, x, group):
    window = jnp.concatenate(
        [field[x + dx, 32 * group : 32 * group + 64, :] for dx in range(3)], axis=0
    )
    return merge_depth(jnp.dot(band[...], window, preferred_element_type=f32), 128)


def second_block(field, band, x, group):
    window = jnp.concatenate(
        [field[x + dx, 128 * group : 128 * group + 160, :] for dx in range(3)], axis=0
    )
    return merge_depth(jnp.dot(band[...], window, preferred_element_type=f32), 128)


def add_row(block, field, band, x, carry, value=None):
    sums, squares = carry
    for group in range(4):
        result = block(field, band, x, group)
        if value is not None:
            value[128 * group : 128 * group + 128, :] = result
        sums = sums + folded(result, 16)
        squares = squares + folded(result * result, 16)
    return sums, squares


def no_sums():
    return jnp.zeros((16, 128), f32), jnp.zeros((16, 128), f32)


def side_rows(block, field, band, rows, gap, value, staged, left):
    def sent(x):
        row = x + jnp.where(x < rows // 2, 0, gap)
        return pltpu.make_async_copy(staged.at[x], value.at[row], left.at[x])

    def step(x, carry):
        row = x + jnp.where(x < rows // 2, 0, gap)
        for group in range(4):
            staged[x, 128 * group : 128 * group + 128, :] = block(field, band, row, group)
        sent(x).start()
        return carry

    lax.fori_loop(0, rows, step, 0, unroll=2)
    for x in range(rows):
        sent(x).wait()


def bands_kernel(taps_one, taps_two, taps_three, one, two, three):
    fill_band(taps_one, one, 4, 16)
    fill_band(taps_two, two, 16, 16)
    fill_band(taps_three, three, 16, 32)


def first_near_kernel(place, near, own, band, partial, field):
    put_volume(own, range(4), field, 4)
    put_sides(place, near, None, 1, field)
    carry = no_sums()
    for x in range(3):
        carry = add_row(first_block, field, band, 4 - (place[0] & 1) + x, carry)
    partial[0], partial[1] = carry


def first_sums_kernel(place, across, own, band, partial, stats, field):
    put_volume(own, range(4), field, 4)
    put_sides(place, None, across, 1, field)
    edge = 3 + 3 * (place[0] & 1)
    put_stats(stats, *add_row(first_block, field, band, edge, (partial[0], partial[1])))


def first_rows_kernel(place, near, across, own, band, value, field, staged, left):
    put_volume(own, range(4), field, 4)
    put_sides(place, near, across, 4, field)
    side_rows(first_block, field, band, 10, 0, value, staged, left)


def put_first(count, place, source, raw, arrived, before, offset, field, rows):
    copies = [pltpu.make_async_copy(source.at[x], raw.at[x], arrived.at[x]) for x in rows]
    for copy in copies:
        copy.start()
    factors = row_factors(before, offset, 16, count * 4 * 32 * 256)
    start = place[0] * 4 - 3
    for x, copy in zip(rows, copies):
        copy.wait()
        inside = jnp.logical_and(start + x >= 0, start + x < count * 4)
        field[x, 0:16, :] = jnp.zeros((16, 256), bf16)
        field[x, 528:544, :] = jnp.zeros((16, 256), bf16)
        for group in range(4):
            active = normed(raw[x, 128 * group : 128 * group + 128, :], factors)
            active = jnp.where(inside, active, 0.0).astype(bf16)
            field[x, 16 + 128 * group : 144 + 128 * group, :] = active


def second_own_kernel(
    count, place, source, before, offset, band, value, stats, raw, arrived, field
):
    put_first(count, place, source, raw, arrived, before, offset, field, range(2, 8))
    carry = no_sums()
    for x in range(4):
        carry = add_row(second_block, field, band, 2 + x, carry, value.at[x])
    put_stats(stats, *carry)


def second_side_kernel(
    count, place, source, before, offset, band, value, raw, arrived, field, staged, left
):
    put_first(count, place, source, raw, arrived, before, offset, field, (0, 1, 2, 3, 6, 7, 8, 9))
    side_rows(second_block, field, band, 4, 4, value, staged, left)


def third_kernel(
    count, place, own, side, before, offset, band, value, stats, raw, arrived, field
):
    copies = {x: pltpu.make_async_copy(side.at[x], raw.at[x], arrived.at[x]) for x in (0, 1, 6, 7)}
    for copy in copies.values():
        copy.start()
    factors = row_factors(before, offset, 16, count * 4 * 32 * 256)
    halve = jnp.where((iota((256, 128), 0) >> 1) == iota((256, 128), 1), 0.125, 0.0).astype(bf16)
    start = place[0] * 2 - 1
    for x in (1, 2, 0, 3):
        if 2 * x in copies:
            copies[2 * x].wait()
            copies[2 * x + 1].wait()
        inside = jnp.logical_and(start + x >= 0, start + x < count * 2)
        field[x, 0:16, :] = jnp.zeros((16, 128), bf16)
        field[x, 272:288, :] = jnp.zeros((16, 128), bf16)
        for group in range(4):
            total = None
            for half in range(2):
                row = 2 * x + half
                source = raw.at[row] if row in copies else own.at[row - 2]
                active = normed(source[128 * group : 128 * group + 128, :], factors)
                part = jnp.dot(active.astype(bf16), halve, preferred_element_type=f32)
                total = part if total is None else total + part
            total = jnp.sum(total.reshape(4, 2, 16, 128), axis=1).reshape(64, 128)
            total = jnp.where(inside, total, 0.0).astype(bf16)
            field[x, 16 + 64 * group : 80 + 64 * group, :] = total
    sums = jnp.zeros((32, 128), f32)
    squares = jnp.zeros((32, 128), f32)
    for x in range(2):
        window = jnp.concatenate(
            [
                jnp.concatenate([field[x + dx, 128 * group : 128 * group + 160, :] for dx in range(3)], axis=0)
                for group in range(2)
            ],
            axis=1,
        )
        parts = jnp.dot(band[...], window, preferred_element_type=f32)
        for group in range(2):
            result = merge_depth(parts[:, 128 * group : 128 * group + 128], 256)
            value[x, 256 * group : 256 * group + 256, :] = result
            sums = sums + folded(result, 32)
            squares = squares + folded(result * result, 32)
    put_stats(stats, sums, squares)


def middle_kernel(count, raw, near, before, offset, middle, pooled, partner):
    factors = row_factors(before, offset, 32, count * 2 * 16 * 128)
    halve = jnp.where(((iota((64, 512), 1) & 127) >> 1) == iota((64, 512), 0), 0.125, 0.0).astype(bf16)
    for place, (source, target) in enumerate(((raw, middle), (near, partner))):
        for x in range(2):
            for group in range(4):
                active = normed(source[x, 128 * group : 128 * group + 128, :], factors).astype(bf16)
                target[x, 128 * group : 128 * group + 128, :] = active
        for part in range(2):
            cells = jnp.concatenate(
                [
                    jnp.concatenate(
                        [
                            target[x, 64 * y + 32 * side : 64 * y + 32 * side + 32, :]
                            for y in range(4 * part, 4 * part + 4)
                        ],
                        axis=0,
                    )
                    for x in range(2)
                    for side in range(2)
                ],
                axis=1,
            )
            total = lax.dot_general(halve, cells, (((1,), (1,)), ((), ())), preferred_element_type=f32)
            pooled[place, 64 * part : 64 * part + 64, :] = total.astype(bf16)


def unpacked(pooled):
    pooled = pooled.astype(f32)
    return jnp.concatenate(
        [
            pooled[64 * part : 64 * part + 64, 32 * side : 32 * side + 32]
            for part in range(2)
            for side in range(4)
        ],
        axis=0,
    )


def along_depth(value):
    rows = value.shape[0]
    depth = iota(value.shape, 0) & 63
    before = jnp.where(depth == 0, 0.0, pltpu.roll(value, 1, 0))
    after = jnp.where(depth == 63, 0.0, pltpu.roll(value, rows - 1, 0))
    return before, value, after


def merge_side(parts):
    none = jnp.zeros((64, 128), f32)
    return (
        parts[:, 128:256]
        + jnp.concatenate([none, parts[:-64, 0:128]], axis=0)
        + jnp.concatenate([parts[64:, 256:384], none], axis=0)
    )


def put_lane_stats(stats, result):
    count = stats.shape[0]
    line = jnp.concatenate(
        [jnp.sum(result, axis=0, keepdims=True), jnp.sum(result * result, axis=0, keepdims=True)], axis=0
    )
    stats[...] = jnp.broadcast_to(line[None], (count, 2, 128))


def fourth_taps(kernel, dx):
    return [
        jnp.concatenate([kernel[dx * 9 + dy * 3 + dz] for dy in range(3)], axis=1) for dz in range(3)
    ]


def fourth_row(parts, taps):
    window = jnp.concatenate([view.astype(bf16) for part in parts for view in along_depth(part)], axis=1)
    return merge_side(jnp.dot(window, jnp.concatenate(taps, axis=0), preferred_element_type=f32))


def whole_fourth_row(parts, kernel):
    return fourth_row(parts, [tap for dx in range(3) for tap in fourth_taps(kernel, dx)])


def in_order(place, near, across):
    odd = (place[0] & 1) == 1
    return jnp.where(odd, near, across), jnp.where(odd, across, near)


def side_taps(place, kernel, near):
    odd = (place[0] & 1) == 1
    before, after = fourth_taps(kernel, 0), fourth_taps(kernel, 2)
    pairs = zip(before, after) if near else zip(after, before)
    return [jnp.where(odd, one.astype(f32), other.astype(f32)).astype(bf16) for one, other in pairs]


def fourth_near_kernel(place, pooled, kernel, value):
    taps = fourth_taps(kernel, 1) + side_taps(place, kernel, True)
    value[...] = fourth_row((unpacked(pooled[0]), unpacked(pooled[1])), taps)


def fourth_kernel(place, across, kernel, partial, value, stats, passed):
    result = partial[...] + fourth_row((unpacked(across[0]),), side_taps(place, kernel, False))
    value[...] = result
    put_lane_stats(stats, result)
    passed[...] = across[0]


def fourth_across_kernel(place, pooled, across, kernel_four, kernel, side, taps):
    centre, middle, far = unpacked(pooled[0]), unpacked(across[0]), unpacked(across[1])
    low, high = in_order(place, centre, far)
    side[...] = whole_fourth_row((low, middle, high), kernel_four)
    for dx in range(3):
        for dz in range(3):
            row = (dx * 3 + dz) * 128
            for dy in range(3):
                taps[row : row + 128, dy * 128 : dy * 128 + 128] = kernel[dx * 9 + dy * 3 + dz]


def fifth_kernel(
    count, place, pooled, passed, side, raw, before, offset, kernel_four, taps, value, stats, field
):
    low, high = in_order(place, unpacked(passed[...]), unpacked(pooled[0]))
    near = whole_fourth_row((low, unpacked(pooled[1]), high), kernel_four)
    low, high = in_order(place, near, side[...])
    parts = (low, raw[...], high)
    factors = lane_factors(before, offset, count * 8 * 64)
    start = place[0] - 1
    for x, part in enumerate(parts):
        inside = jnp.logical_and(start + x >= 0, start + x < count)
        active = jnp.where(inside, normed(part, factors), 0.0)
        for dz, view in enumerate(along_depth(active)):
            lane = (x * 3 + dz) * 128
            field[:, lane : lane + 128] = view.astype(bf16)
    parts = jnp.dot(field[...], taps[...], preferred_element_type=f32)
    result = merge_side(parts)
    value[...] = result
    put_lane_stats(stats, result)


def decode_kernel(count, place, raw, before, offset, up, middle, decoded):
    factors = lane_factors(before, offset, count * 8 * 64)
    stripe = place[0]
    active = normed(raw[pl.ds(pl.multiple_of(stripe * 64, 64), 64), :], factors).astype(bf16)
    twice = jnp.where((iota((128, 64), 0) >> 1) == iota((128, 64), 1), 1.0, 0.0).astype(bf16)
    active = jnp.dot(twice, active, preferred_element_type=f32).astype(bf16)
    projected = lax.dot_general(up[...], active, (((1,), (1,)), ((), ())), preferred_element_type=f32)
    blocks = []
    for x in range(2):
        own = middle[x, pl.ds(pl.multiple_of(stripe * 64, 64), 64), :].astype(f32)
        for side in range(2):
            merged = jnp.maximum(projected + own[32 * side : 32 * side + 32], 0.0)
            blocks.append(merged.astype(bf16))
    blocks = jnp.concatenate(blocks, axis=0)
    row = iota((128, 128), 0)
    order = jnp.where(((row & 3) * 32 + (row >> 2)) == iota((128, 128), 1), 1.0, 0.0).astype(bf16)
    decoded[...] = jnp.dot(order, blocks, preferred_element_type=f32).astype(bf16)


def shape(dims, kind=f32):
    return jax.ShapeDtypeStruct(dims, kind)


def call(kernel, outs, places, scratch=(), out_places=None, grant=28):
    spaces = {"S": pltpu.SMEM, "V": pltpu.VMEM, "H": pltpu.HBM}

    def specs(letters):
        return tuple(pl.BlockSpec(memory_space=spaces[letter]) for letter in letters)

    single = not isinstance(outs, tuple)
    out_specs = specs(out_places or "V" * (1 if single else len(outs)))
    return pl.pallas_call(
        kernel,
        out_shape=outs,
        in_specs=specs(places),
        out_specs=out_specs[0] if single else out_specs,
        scratch_shapes=list(scratch),
        compiler_params=pltpu.CompilerParams(vmem_limit_bytes=grant * 1024 * 1024),
        cost_estimate=pl.CostEstimate(flops=1 << 30, bytes_accessed=1 << 22, transcendentals=0),
    )


def swap(stats):
    return lax.all_to_all(stats, "gx", 0, 0)


def bind(kernel, count):
    def bound(*refs):
        kernel(count, *refs)

    return bound


def shards(
    volume,
    weight_one,
    offset_one,
    weight_two,
    offset_two,
    weight_three,
    offset_three,
    weight_four,
    offset_four,
    weight_five,
    offset_five,
    weight_up,
):
    count = lax.axis_size("gx")
    place = lax.axis_index("gx").astype(jnp.int32)[None]
    stripe = lax.axis_index("yz").astype(jnp.int32)[None]

    def swapped(block, first):
        pairs = [(i, i + 1) for i in range(first, count - 1, 2)]
        return lax.ppermute(block, "gx", pairs + [(target, source) for source, target in pairs])

    def line(offset):
        return jnp.pad(offset, (0, 128 - offset.shape[0]))[None]

    statistics = shape((count, 2, 128))
    large, medium, small = 51, 51, 48
    arrivals = pltpu.SemaphoreType.DMA
    band_one, band_two, band_three = call(
        bands_kernel,
        (shape((384, 192), bf16), shape((384, 480), bf16), shape((768, 480), bf16)),
        "VVV",
    )(tap_rows(weight_one, 3, 16), tap_rows(weight_two, 0, 10), tap_rows(weight_three, 0, 10))

    block = jnp.transpose(volume, (1, 2, 0, 3)).reshape(4, 16, 256)
    own = lax.all_to_all(jnp.broadcast_to(block[None], (8, 4, 16, 256)), "yz", 0, 0)
    across, near = swapped(own, 1), swapped(own, 0)

    def staged(rows):
        return (pltpu.VMEM((rows, 512, 256), f32), arrivals((rows,)))

    inputs = (place, near, across, own, band_one)
    field = (pltpu.VMEM((12, 160, 256), bf16),)
    partial = call(first_near_kernel, shape((2, 16, 128)), "SVVV", field)(place, near, own, band_one)
    stats = call(first_sums_kernel, statistics, "SVVVV", field, grant=large)(
        place, across, own, band_one, partial
    )
    rows = call(
        first_rows_kernel, shape((10, 512, 256)), "SVVVV", (*field, *staged(10)), "H", large
    )(*inputs)

    inputs = (place, rows, swap(stats), line(offset_one), band_two)
    field = (*staged(10), pltpu.VMEM((10, 544, 256), bf16))
    raw, stats = call(
        bind(second_own_kernel, count),
        (shape((4, 512, 256)), statistics),
        "SHVVV",
        field,
        grant=large,
    )(*inputs)
    side = call(
        bind(second_side_kernel, count),
        shape((8, 512, 256)),
        "SHVVV",
        (*field, *staged(4)),
        "H",
        medium,
    )(*inputs)

    raw, stats = call(
        bind(third_kernel, count),
        (shape((2, 512, 128)), statistics),
        "SVHVVV",
        (*staged(8), pltpu.VMEM((4, 288, 128), bf16)),
        grant=small,
    )(place, raw, side, swap(stats), line(offset_two), band_three)

    middle, pooled = call(
        bind(middle_kernel, count),
        (shape((2, 512, 128), bf16), shape((2, 128, 128), bf16)),
        "VVVV",
        (pltpu.VMEM((2, 512, 128), bf16),),
    )(raw, swapped(raw, 0), swap(stats), line(offset_three))
    across = swapped(pooled, 1)
    taps_four = weight_four.reshape(27, 32, 128)
    taps_five = weight_five.reshape(27, 128, 128)
    partial = call(fourth_near_kernel, shape((512, 128)), "SVV")(place, pooled, taps_four)
    raw, stats, passed = call(
        fourth_kernel,
        (shape((512, 128)), statistics, shape((128, 128), bf16)),
        "SVVV",
    )(place, across, taps_four, partial)
    side, taps_five = call(
        fourth_across_kernel, (shape((512, 128)), shape((1152, 384), bf16)), "SVVVV"
    )(place, pooled, across, taps_four, taps_five)
    raw, stats = call(
        bind(fifth_kernel, count),
        (shape((512, 128)), statistics),
        "SVVVVVVVV",
        (pltpu.VMEM((512, 1152), bf16),),
    )(
        place,
        pooled,
        swapped(passed, 0),
        side,
        raw,
        swap(stats),
        offset_four[None],
        taps_four,
        taps_five,
    )
    decoded = call(
        bind(decode_kernel, count),
        shape((128, 128), bf16),
        "SVVVVV",
    )(stripe, raw, swap(stats), offset_five[None], weight_up.T, middle)
    return decoded.reshape(32, 2, 2, 128)


def solution(mesh):
    return jax.shard_map(
        shards,
        mesh=mesh,
        in_specs=(P(None, "gx", "yz", None), P(), P(), P(), P(), P(), P(), P(), P(), P(), P(), P()),
        out_specs=P(None, "gx", "yz", None),
        check_vma=False,
    )
```

```python
import jax
import jax.numpy as jnp
from jax import lax
from jax.experimental import pallas as pl
from jax.experimental.pallas import tpu as pltpu
from jax.sharding import PartitionSpec as P

epsilon = 1e-05
f32 = jnp.float32
bf16 = jnp.bfloat16


def iota(shape, dim):
    return lax.broadcasted_iota(jnp.int32, shape, dim)


def tap_rows(kernel, before, slots):
    taps = jnp.transpose(kernel, (2, 4, 0, 1, 3)).astype(f32)
    taps = jnp.pad(taps, ((0, 0), (0, 0), (0, 0), (before, slots - 3 - before), (0, 0)))
    out, inner = kernel.shape[4], kernel.shape[3]
    taps = taps.reshape(3 * out, 3 * slots * inner)
    return jnp.pad(taps, ((0, 0), (0, -taps.shape[1] % 128)))


def fill_band(taps, band, step, out):
    depth = band.shape[1]
    base = taps[...]
    for row in range(8):
        moved = base if row == 0 else pltpu.roll(base, row * step, 1)
        for dz in range(3):
            start = (dz * 8 + row) * out
            band[start : start + out, :] = moved[dz * out : (dz + 1) * out, :depth].astype(bf16)


def merge_depth(parts, rows):
    width = parts.shape[1]
    lane = iota((rows, width), 1)
    before = jnp.where(lane == 0, 0.0, pltpu.roll(parts[:rows], 1, 1))
    after = jnp.where(lane == width - 1, 0.0, pltpu.roll(parts[2 * rows :], width - 1, 1))
    return parts[rows : 2 * rows] + before + after


def put_stats(stats, sums, squares):
    count = stats.shape[0]
    none = jnp.zeros((128 - sums.shape[0], 128), f32)
    lines = [
        jnp.sum(jnp.concatenate([part, none], axis=0).T, axis=0, keepdims=True) for part in (sums, squares)
    ]
    stats[...] = jnp.broadcast_to(jnp.concatenate(lines, axis=0)[None], (count, 2, 128))


def folded(value, channels):
    width = value.shape[1]
    total = value[:, :128]
    for start in range(128, width, 128):
        total = total + value[:, start : start + 128]
    return jnp.sum(total.reshape(-1, channels, 128), axis=0)


def row_factors(stats, offset, channels, cells):
    total = jnp.sum(stats[...], axis=0)
    lane = iota((128, 128), 1)
    same = (iota((128, 128), 0) & (channels - 1)) == (lane & (channels - 1))

    def column(line, keep):
        return jnp.sum(jnp.where(keep, line, 0.0), axis=1, keepdims=True)

    average = column(total[0:1], same) / cells
    variance = column(total[1:2], same) / cells - average * average
    shift = column(offset[...], jnp.logical_and(same, lane < channels))
    return average, lax.rsqrt(variance + epsilon), shift


def lane_factors(stats, offset, cells):
    total = jnp.sum(stats[...], axis=0)
    average = total[0:1] / cells
    variance = total[1:2] / cells - average * average
    return average, lax.rsqrt(variance + epsilon), offset[...]


def normed(value, factors):
    average, inverse, shift = factors
    return jnp.maximum((value - average) * inverse + shift, 0.0)


def put_volume(part, rows, field, begin):
    for x in rows:
        field[begin + x, 0:16, :] = jnp.zeros((16, 256), bf16)
        field[begin + x, 144:160, :] = jnp.zeros((16, 256), bf16)
        for block in range(8):
            field[begin + x, 16 + 16 * block : 32 + 16 * block, :] = part[block, x]


def put_sides(place, near, across, rows, field):
    odd = place[0] & 1

    def put(low, high):
        if low is not None:
            put_volume(low, range(4 - rows, 4), field, 0)
        if high is not None:
            put_volume(high, range(rows), field, 8)

    pl.when(odd == 0)(lambda: put(across, near))
    pl.when(odd == 1)(lambda: put(near, across))


def first_block(field, band, x, group):
    window = jnp.concatenate(
        [field[x + dx, 32 * group : 32 * group + 64, :] for dx in range(3)], axis=0
    )
    return merge_depth(jnp.dot(band[...], window, preferred_element_type=f32), 128)


def second_block(field, band, x, group):
    window = jnp.concatenate(
        [field[x + dx, 128 * group : 128 * group + 160, :] for dx in range(3)], axis=0
    )
    return merge_depth(jnp.dot(band[...], window, preferred_element_type=f32), 128)


def add_row(block, field, band, x, carry, value=None):
    sums, squares = carry
    for group in range(4):
        result = block(field, band, x, group)
        if value is not None:
            value[128 * group : 128 * group + 128, :] = result
        sums = sums + folded(result, 16)
        squares = squares + folded(result * result, 16)
    return sums, squares


def no_sums():
    return jnp.zeros((16, 128), f32), jnp.zeros((16, 128), f32)


def side_rows(block, field, band, rows, gap, value, staged, left):
    def sent(x):
        row = x + jnp.where(x < rows // 2, 0, gap)
        return pltpu.make_async_copy(staged.at[x], value.at[row], left.at[x])

    def step(x, carry):
        row = x + jnp.where(x < rows // 2, 0, gap)
        for group in range(4):
            staged[x, 128 * group : 128 * group + 128, :] = block(field, band, row, group)
        sent(x).start()
        return carry

    lax.fori_loop(0, rows, step, 0, unroll=2)
    for x in range(rows):
        sent(x).wait()


def bands_kernel(taps_one, taps_two, taps_three, one, two, three):
    fill_band(taps_one, one, 4, 16)
    fill_band(taps_two, two, 16, 16)
    fill_band(taps_three, three, 16, 32)


def first_across_kernel(place, across, own, band, partial, field):
    put_volume(own, range(4), field, 4)
    put_sides(place, None, across, 1, field)
    carry = no_sums()
    for x in range(3):
        carry = add_row(first_block, field, band, 3 + (place[0] & 1) + x, carry)
    partial[0], partial[1] = carry


def first_sums_kernel(place, near, own, band, partial, stats, field):
    put_volume(own, range(4), field, 4)
    put_sides(place, near, None, 1, field)
    edge = 6 - 3 * (place[0] & 1)
    put_stats(stats, *add_row(first_block, field, band, edge, (partial[0], partial[1])))


def first_rows_kernel(place, near, across, own, band, value, field, staged, left):
    put_volume(own, range(4), field, 4)
    put_sides(place, near, across, 4, field)
    side_rows(first_block, field, band, 10, 0, value, staged, left)


def put_first(count, place, source, raw, arrived, before, offset, field, rows):
    copies = [pltpu.make_async_copy(source.at[x], raw.at[x], arrived.at[x]) for x in rows]
    for copy in copies:
        copy.start()
    factors = row_factors(before, offset, 16, count * 4 * 32 * 256)
    start = place[0] * 4 - 3
    for x, copy in zip(rows, copies):
        copy.wait()
        inside = jnp.logical_and(start + x >= 0, start + x < count * 4)
        field[x, 0:16, :] = jnp.zeros((16, 256), bf16)
        field[x, 528:544, :] = jnp.zeros((16, 256), bf16)
        for group in range(4):
            active = normed(raw[x, 128 * group : 128 * group + 128, :], factors)
            active = jnp.where(inside, active, 0.0).astype(bf16)
            field[x, 16 + 128 * group : 144 + 128 * group, :] = active


def second_own_kernel(
    count, place, source, before, offset, band, value, stats, raw, arrived, field
):
    put_first(count, place, source, raw, arrived, before, offset, field, range(2, 8))
    carry = no_sums()
    for x in range(4):
        carry = add_row(second_block, field, band, 2 + x, carry, value.at[x])
    put_stats(stats, *carry)


def second_side_kernel(
    count, place, source, before, offset, band, value, raw, arrived, field, staged, left
):
    put_first(count, place, source, raw, arrived, before, offset, field, (0, 1, 2, 3, 6, 7, 8, 9))
    side_rows(second_block, field, band, 4, 4, value, staged, left)


def third_kernel(
    count, place, own, side, before, offset, band, value, stats, raw, arrived, field
):
    copies = {x: pltpu.make_async_copy(side.at[x], raw.at[x], arrived.at[x]) for x in (0, 1, 6, 7)}
    for copy in copies.values():
        copy.start()
    factors = row_factors(before, offset, 16, count * 4 * 32 * 256)
    halve = jnp.where((iota((256, 128), 0) >> 1) == iota((256, 128), 1), 0.125, 0.0).astype(bf16)
    start = place[0] * 2 - 1
    for x in (1, 2, 0, 3):
        if 2 * x in copies:
            copies[2 * x].wait()
            copies[2 * x + 1].wait()
        inside = jnp.logical_and(start + x >= 0, start + x < count * 2)
        field[x, 0:16, :] = jnp.zeros((16, 128), bf16)
        field[x, 272:288, :] = jnp.zeros((16, 128), bf16)
        for group in range(4):
            total = None
            for half in range(2):
                row = 2 * x + half
                source = raw.at[row] if row in copies else own.at[row - 2]
                active = normed(source[128 * group : 128 * group + 128, :], factors)
                part = jnp.dot(active.astype(bf16), halve, preferred_element_type=f32)
                total = part if total is None else total + part
            total = jnp.sum(total.reshape(4, 2, 16, 128), axis=1).reshape(64, 128)
            total = jnp.where(inside, total, 0.0).astype(bf16)
            field[x, 16 + 64 * group : 80 + 64 * group, :] = total
    sums = jnp.zeros((32, 128), f32)
    squares = jnp.zeros((32, 128), f32)
    for x in range(2):
        window = jnp.concatenate(
            [
                jnp.concatenate([field[x + dx, 128 * group : 128 * group + 160, :] for dx in range(3)], axis=0)
                for group in range(2)
            ],
            axis=1,
        )
        parts = jnp.dot(band[...], window, preferred_element_type=f32)
        for group in range(2):
            result = merge_depth(parts[:, 128 * group : 128 * group + 128], 256)
            value[x, 256 * group : 256 * group + 256, :] = result
            sums = sums + folded(result, 32)
            squares = squares + folded(result * result, 32)
    put_stats(stats, sums, squares)


def put_middle(count, raw, before, offset, middle, pooled):
    factors = row_factors(before, offset, 32, count * 2 * 16 * 128)
    halve = jnp.where(((iota((64, 512), 1) & 127) >> 1) == iota((64, 512), 0), 0.125, 0.0).astype(bf16)
    for x in range(2):
        for group in range(4):
            active = normed(raw[x, 128 * group : 128 * group + 128, :], factors).astype(bf16)
            middle[x, 128 * group : 128 * group + 128, :] = active
    for part in range(2):
        cells = jnp.concatenate(
            [
                jnp.concatenate(
                    [
                        middle[x, 64 * y + 32 * side : 64 * y + 32 * side + 32, :]
                        for y in range(4 * part, 4 * part + 4)
                    ],
                    axis=0,
                )
                for x in range(2)
                for side in range(2)
            ],
            axis=1,
        )
        total = lax.dot_general(halve, cells, (((1,), (1,)), ((), ())), preferred_element_type=f32)
        pooled[64 * part : 64 * part + 64, :] = total.astype(bf16)


def middle_near_kernel(count, raw, before, offset, own, pooled, middle):
    pooled[0] = own[...]
    put_middle(count, raw, before, offset, middle, pooled.at[1])


def unpacked(pooled):
    pooled = pooled.astype(f32)
    return jnp.concatenate(
        [
            pooled[64 * part : 64 * part + 64, 32 * side : 32 * side + 32]
            for part in range(2)
            for side in range(4)
        ],
        axis=0,
    )


def along_depth(value):
    rows = value.shape[0]
    depth = iota(value.shape, 0) & 63
    before = jnp.where(depth == 0, 0.0, pltpu.roll(value, 1, 0))
    after = jnp.where(depth == 63, 0.0, pltpu.roll(value, rows - 1, 0))
    return before, value, after


def merge_side(parts):
    none = jnp.zeros((64, 128), f32)
    return (
        parts[:, 128:256]
        + jnp.concatenate([none, parts[:-64, 0:128]], axis=0)
        + jnp.concatenate([parts[64:, 256:384], none], axis=0)
    )


def put_lane_stats(stats, result):
    count = stats.shape[0]
    line = jnp.concatenate(
        [jnp.sum(result, axis=0, keepdims=True), jnp.sum(result * result, axis=0, keepdims=True)], axis=0
    )
    stats[...] = jnp.broadcast_to(line[None], (count, 2, 128))


def fourth_taps(kernel, dx):
    return [
        jnp.concatenate([kernel[dx * 9 + dy * 3 + dz] for dy in range(3)], axis=1) for dz in range(3)
    ]


def fourth_row(parts, taps):
    window = jnp.concatenate([view.astype(bf16) for part in parts for view in along_depth(part)], axis=1)
    return merge_side(jnp.dot(window, jnp.concatenate(taps, axis=0), preferred_element_type=f32))


def whole_fourth_row(parts, kernel):
    return fourth_row(parts, [tap for dx in range(3) for tap in fourth_taps(kernel, dx)])


def in_order(place, near, across):
    odd = (place[0] & 1) == 1
    return jnp.where(odd, near, across), jnp.where(odd, across, near)


def side_taps(place, kernel, near):
    odd = (place[0] & 1) == 1
    before, after = fourth_taps(kernel, 0), fourth_taps(kernel, 2)
    pairs = zip(before, after) if near else zip(after, before)
    return [jnp.where(odd, one.astype(f32), other.astype(f32)).astype(bf16) for one, other in pairs]


def fourth_near_kernel(place, pooled, kernel, value):
    taps = fourth_taps(kernel, 1) + side_taps(place, kernel, True)
    value[...] = fourth_row((unpacked(pooled[0]), unpacked(pooled[1])), taps)


def fourth_kernel(place, across, kernel, partial, value, stats, passed):
    result = partial[...] + fourth_row((unpacked(across[0]),), side_taps(place, kernel, False))
    value[...] = result
    put_lane_stats(stats, result)
    passed[...] = across[0]


def fourth_side_kernel(place, pooled, across, kernel_four, kernel, near, side, taps):
    centre, middle, far = unpacked(pooled[0]), unpacked(across[0]), unpacked(across[1])
    low, high = in_order(place, centre, far)
    side[...] = whole_fourth_row((low, middle, high), kernel_four)
    near_taps = fourth_taps(kernel_four, 1) + side_taps(place, kernel_four, False)
    near[...] = fourth_row((unpacked(pooled[1]), centre), near_taps)
    for dx in range(3):
        for dz in range(3):
            row = (dx * 3 + dz) * 128
            for dy in range(3):
                taps[row : row + 128, dy * 128 : dy * 128 + 128] = kernel[dx * 9 + dy * 3 + dz]


def fifth_kernel(
    count, place, passed, near, side, raw, before, offset, kernel_four, taps, value, stats, field
):
    near = near[...] + fourth_row((unpacked(passed[...]),), side_taps(place, kernel_four, True))
    low, high = in_order(place, near, side[...])
    parts = (low, raw[...], high)
    factors = lane_factors(before, offset, count * 8 * 64)
    start = place[0] - 1
    for x, part in enumerate(parts):
        inside = jnp.logical_and(start + x >= 0, start + x < count)
        active = jnp.where(inside, normed(part, factors), 0.0)
        for dz, view in enumerate(along_depth(active)):
            lane = (x * 3 + dz) * 128
            field[:, lane : lane + 128] = view.astype(bf16)
    parts = jnp.dot(field[...], taps[...], preferred_element_type=f32)
    result = merge_side(parts)
    value[...] = result
    put_lane_stats(stats, result)


def decode_kernel(count, place, raw, before, offset, up, middle, decoded):
    factors = lane_factors(before, offset, count * 8 * 64)
    stripe = place[0]
    active = normed(raw[pl.ds(pl.multiple_of(stripe * 64, 64), 64), :], factors).astype(bf16)
    twice = jnp.where((iota((128, 64), 0) >> 1) == iota((128, 64), 1), 1.0, 0.0).astype(bf16)
    active = jnp.dot(twice, active, preferred_element_type=f32).astype(bf16)
    projected = lax.dot_general(up[...], active, (((1,), (1,)), ((), ())), preferred_element_type=f32)
    blocks = []
    for x in range(2):
        own = middle[x, pl.ds(pl.multiple_of(stripe * 64, 64), 64), :].astype(f32)
        for side in range(2):
            merged = jnp.maximum(projected + own[32 * side : 32 * side + 32], 0.0)
            blocks.append(merged.astype(bf16))
    blocks = jnp.concatenate(blocks, axis=0)
    row = iota((128, 128), 0)
    order = jnp.where(((row & 3) * 32 + (row >> 2)) == iota((128, 128), 1), 1.0, 0.0).astype(bf16)
    decoded[...] = jnp.dot(order, blocks, preferred_element_type=f32).astype(bf16)


def shape(dims, kind=f32):
    return jax.ShapeDtypeStruct(dims, kind)


def call(kernel, outs, places, scratch=(), out_places=None, grant=28, flops=1 << 30):
    spaces = {"S": pltpu.SMEM, "V": pltpu.VMEM, "H": pltpu.HBM}

    def specs(letters):
        return tuple(pl.BlockSpec(memory_space=spaces[letter]) for letter in letters)

    single = not isinstance(outs, tuple)
    out_specs = specs(out_places or "V" * (1 if single else len(outs)))
    return pl.pallas_call(
        kernel,
        out_shape=outs,
        in_specs=specs(places),
        out_specs=out_specs[0] if single else out_specs,
        scratch_shapes=list(scratch),
        compiler_params=pltpu.CompilerParams(vmem_limit_bytes=grant * 1024 * 1024),
        cost_estimate=pl.CostEstimate(flops=flops, bytes_accessed=flops >> 8, transcendentals=0),
    )


def swap(stats):
    return lax.all_to_all(stats, "gx", 0, 0)


def bind(kernel, count):
    def bound(*refs):
        kernel(count, *refs)

    return bound


def shards(
    volume,
    weight_one,
    offset_one,
    weight_two,
    offset_two,
    weight_three,
    offset_three,
    weight_four,
    offset_four,
    weight_five,
    offset_five,
    weight_up,
):
    count = lax.axis_size("gx")
    place = lax.axis_index("gx").astype(jnp.int32)[None]
    stripe = lax.axis_index("yz").astype(jnp.int32)[None]

    def swapped(block, first):
        pairs = [(i, i + 1) for i in range(first, count - 1, 2)]
        return lax.ppermute(block, "gx", pairs + [(target, source) for source, target in pairs])

    def line(offset):
        return jnp.pad(offset, (0, 128 - offset.shape[0]))[None]

    statistics = shape((count, 2, 128))
    large, medium, small = 51, 51, 48
    arrivals = pltpu.SemaphoreType.DMA
    block = jnp.transpose(volume, (1, 2, 0, 3)).reshape(4, 16, 256)
    own = lax.all_to_all(jnp.broadcast_to(block[None], (8, 4, 16, 256)), "yz", 0, 0)
    across = swapped(own, 1)
    band_one, band_two, band_three = call(
        bands_kernel,
        (shape((384, 192), bf16), shape((384, 480), bf16), shape((768, 480), bf16)),
        "VVV",
    )(tap_rows(weight_one, 3, 16), tap_rows(weight_two, 0, 10), tap_rows(weight_three, 0, 10))
    near = swapped(own, 0)

    def staged(rows):
        return (pltpu.VMEM((rows, 512, 256), f32), arrivals((rows,)))

    inputs = (place, near, across, own, band_one)
    field = (pltpu.VMEM((12, 160, 256), bf16),)
    partial = call(first_across_kernel, shape((2, 16, 128)), "SVVV", field)(place, across, own, band_one)
    stats = call(first_sums_kernel, statistics, "SVVVV", field, grant=large)(
        place, near, own, band_one, partial
    )
    rows = call(
        first_rows_kernel, shape((10, 512, 256)), "SVVVV", (*field, *staged(10)), "H", large
    )(*inputs)

    inputs = (place, rows, swap(stats), line(offset_one), band_two)
    field = (*staged(10), pltpu.VMEM((10, 544, 256), bf16))
    raw, stats = call(
        bind(second_own_kernel, count),
        (shape((4, 512, 256)), statistics),
        "SHVVV",
        field,
        grant=large,
    )(*inputs)
    side = call(
        bind(second_side_kernel, count),
        shape((8, 512, 256)),
        "SHVVV",
        (*field, *staged(4)),
        "H",
        medium,
    )(*inputs)

    raw, stats = call(
        bind(third_kernel, count),
        (shape((2, 512, 128)), statistics),
        "SVHVVV",
        (*staged(8), pltpu.VMEM((4, 288, 128), bf16)),
        grant=small,
    )(place, raw, side, swap(stats), line(offset_two), band_three)

    near, sums = swapped(raw, 0), swap(stats)
    middle, pooled = call(
        bind(put_middle, count),
        (shape((2, 512, 128), bf16), shape((128, 128), bf16)),
        "VVV",
        flops=1 << 34,
    )(raw, sums, line(offset_three))
    pooled = call(
        bind(middle_near_kernel, count),
        shape((2, 128, 128), bf16),
        "VVVV",
        (pltpu.VMEM((2, 512, 128), bf16),),
    )(near, sums, line(offset_three), pooled)
    across = swapped(pooled, 1)
    taps_four = weight_four.reshape(27, 32, 128)
    taps_five = weight_five.reshape(27, 128, 128)
    partial = call(fourth_near_kernel, shape((512, 128)), "SVV")(place, pooled, taps_four)
    raw, stats, passed = call(
        fourth_kernel,
        (shape((512, 128)), statistics, shape((128, 128), bf16)),
        "SVVV",
    )(place, across, taps_four, partial)
    near, side, taps_five = call(
        fourth_side_kernel, (shape((512, 128)), shape((512, 128)), shape((1152, 384), bf16)), "SVVVV"
    )(place, pooled, across, taps_four, taps_five)
    raw, stats = call(
        bind(fifth_kernel, count),
        (shape((512, 128)), statistics),
        "SVVVVVVVV",
        (pltpu.VMEM((512, 1152), bf16),),
    )(
        place,
        swapped(passed, 0),
        near,
        side,
        raw,
        swap(stats),
        offset_four[None],
        taps_four,
        taps_five,
    )
    decoded = call(
        bind(decode_kernel, count),
        shape((128, 128), bf16),
        "SVVVVV",
    )(stripe, raw, swap(stats), offset_five[None], weight_up.T, middle)
    return decoded.reshape(32, 2, 2, 128)


def solution(mesh):
    return jax.shard_map(
        shards,
        mesh=mesh,
        in_specs=(P(None, "gx", "yz", None), P(), P(), P(), P(), P(), P(), P(), P(), P(), P(), P()),
        out_specs=P(None, "gx", "yz", None),
        check_vma=False,
    )
```

```python
import jax
import jax.numpy as jnp
from jax import lax
from jax.experimental import pallas as pl
from jax.experimental.pallas import tpu as pltpu
from jax.sharding import PartitionSpec as P

epsilon = 1e-05
f32 = jnp.float32
bf16 = jnp.bfloat16


def iota(shape, dim):
    return lax.broadcasted_iota(jnp.int32, shape, dim)


def tap_rows(kernel, before, slots):
    taps = jnp.transpose(kernel, (2, 4, 0, 1, 3)).astype(f32)
    taps = jnp.pad(taps, ((0, 0), (0, 0), (0, 0), (before, slots - 3 - before), (0, 0)))
    out, inner = kernel.shape[4], kernel.shape[3]
    taps = taps.reshape(3 * out, 3 * slots * inner)
    return jnp.pad(taps, ((0, 0), (0, -taps.shape[1] % 128)))


def fill_band(taps, band, step, out):
    depth = band.shape[1]
    base = taps[...]
    for row in range(8):
        moved = base if row == 0 else pltpu.roll(base, row * step, 1)
        for dz in range(3):
            start = (dz * 8 + row) * out
            band[start : start + out, :] = moved[dz * out : (dz + 1) * out, :depth].astype(bf16)


def merge_depth(parts, rows):
    width = parts.shape[1]
    lane = iota((rows, width), 1)
    before = jnp.where(lane == 0, 0.0, pltpu.roll(parts[:rows], 1, 1))
    after = jnp.where(lane == width - 1, 0.0, pltpu.roll(parts[2 * rows :], width - 1, 1))
    return parts[rows : 2 * rows] + before + after


def put_stats(stats, sums, squares):
    count = stats.shape[0]
    none = jnp.zeros((128 - sums.shape[0], 128), f32)
    lines = [
        jnp.sum(jnp.concatenate([part, none], axis=0).T, axis=0, keepdims=True) for part in (sums, squares)
    ]
    stats[...] = jnp.broadcast_to(jnp.concatenate(lines, axis=0)[None], (count, 2, 128))


def folded(value, channels):
    width = value.shape[1]
    total = value[:, :128]
    for start in range(128, width, 128):
        total = total + value[:, start : start + 128]
    return jnp.sum(total.reshape(-1, channels, 128), axis=0)


def row_factors(stats, offset, channels, cells):
    total = jnp.sum(stats[...], axis=0)
    lane = iota((128, 128), 1)
    same = (iota((128, 128), 0) & (channels - 1)) == (lane & (channels - 1))

    def column(line, keep):
        return jnp.sum(jnp.where(keep, line, 0.0), axis=1, keepdims=True)

    average = column(total[0:1], same) / cells
    variance = column(total[1:2], same) / cells - average * average
    shift = column(offset[...], jnp.logical_and(same, lane < channels))
    return average, lax.rsqrt(variance + epsilon), shift


def lane_factors(stats, offset, cells):
    total = jnp.sum(stats[...], axis=0)
    average = total[0:1] / cells
    variance = total[1:2] / cells - average * average
    return average, lax.rsqrt(variance + epsilon), offset[...]


def normed(value, factors):
    average, inverse, shift = factors
    return jnp.maximum((value - average) * inverse + shift, 0.0)


def put_volume(part, rows, field, begin):
    for x in rows:
        field[begin + x, 0:16, :] = jnp.zeros((16, 256), bf16)
        field[begin + x, 144:160, :] = jnp.zeros((16, 256), bf16)
        for block in range(8):
            field[begin + x, 16 + 16 * block : 32 + 16 * block, :] = part[block, x]


def put_sides(place, near, across, rows, field):
    odd = place[0] & 1

    def put(low, high):
        if low is not None:
            put_volume(low, range(4 - rows, 4), field, 0)
        if high is not None:
            put_volume(high, range(rows), field, 8)

    pl.when(odd == 0)(lambda: put(across, near))
    pl.when(odd == 1)(lambda: put(near, across))


def first_block(field, band, x, group):
    window = jnp.concatenate(
        [field[x + dx, 32 * group : 32 * group + 64, :] for dx in range(3)], axis=0
    )
    return merge_depth(jnp.dot(band[...], window, preferred_element_type=f32), 128)


def second_block(field, band, x, group):
    window = jnp.concatenate(
        [field[x + dx, 128 * group : 128 * group + 160, :] for dx in range(3)], axis=0
    )
    return merge_depth(jnp.dot(band[...], window, preferred_element_type=f32), 128)


def add_row(block, field, band, x, carry, value=None):
    sums, squares = carry
    for group in range(4):
        result = block(field, band, x, group)
        if value is not None:
            value[128 * group : 128 * group + 128, :] = result
        sums = sums + folded(result, 16)
        squares = squares + folded(result * result, 16)
    return sums, squares


def no_sums():
    return jnp.zeros((16, 128), f32), jnp.zeros((16, 128), f32)


def side_rows(block, field, band, rows, gap, value, staged, left):
    def sent(x):
        row = x + jnp.where(x < rows // 2, 0, gap)
        return pltpu.make_async_copy(staged.at[x], value.at[row], left.at[x])

    def step(x, carry):
        row = x + jnp.where(x < rows // 2, 0, gap)
        for group in range(4):
            staged[x, 128 * group : 128 * group + 128, :] = block(field, band, row, group)
        sent(x).start()
        return carry

    lax.fori_loop(0, rows, step, 0, unroll=2)
    for x in range(rows):
        sent(x).wait()


def bands_kernel(taps_one, taps_two, taps_three, one, two, three):
    fill_band(taps_one, one, 4, 16)
    fill_band(taps_two, two, 16, 16)
    fill_band(taps_three, three, 16, 32)


def first_across_kernel(place, across, own, band, partial, field):
    put_volume(own, range(4), field, 4)
    put_sides(place, None, across, 1, field)
    carry = no_sums()
    for x in range(3):
        carry = add_row(first_block, field, band, 3 + (place[0] & 1) + x, carry)
    partial[0], partial[1] = carry


def first_sums_kernel(place, near, own, band, partial, stats, field):
    put_volume(own, range(4), field, 4)
    put_sides(place, near, None, 1, field)
    edge = 6 - 3 * (place[0] & 1)
    put_stats(stats, *add_row(first_block, field, band, edge, (partial[0], partial[1])))


def first_rows_kernel(place, near, across, own, band, value, field, staged, left):
    put_volume(own, range(4), field, 4)
    put_sides(place, near, across, 4, field)
    side_rows(first_block, field, band, 10, 0, value, staged, left)


def put_first(count, place, source, raw, arrived, before, offset, field, rows):
    copies = [pltpu.make_async_copy(source.at[x], raw.at[x], arrived.at[x]) for x in rows]
    for copy in copies:
        copy.start()
    factors = row_factors(before, offset, 16, count * 4 * 32 * 256)
    start = place[0] * 4 - 3
    for x, copy in zip(rows, copies):
        copy.wait()
        inside = jnp.logical_and(start + x >= 0, start + x < count * 4)
        field[x, 0:16, :] = jnp.zeros((16, 256), bf16)
        field[x, 528:544, :] = jnp.zeros((16, 256), bf16)
        for group in range(4):
            active = normed(raw[x, 128 * group : 128 * group + 128, :], factors)
            active = jnp.where(inside, active, 0.0).astype(bf16)
            field[x, 16 + 128 * group : 144 + 128 * group, :] = active


def second_own_kernel(
    count, place, source, before, offset, band, value, stats, raw, arrived, field, staged, left
):
    put_first(count, place, source, raw, arrived, before, offset, field, range(2, 8))
    carry, copies = no_sums(), []
    for x in range(4):
        carry = add_row(second_block, field, band, 2 + x, carry, staged.at[x])
        copies.append(pltpu.make_async_copy(staged.at[x], value.at[2 + x], left.at[x]))
        copies[x].start()
    put_stats(stats, *carry)
    for copy in copies:
        copy.wait()


def second_side_kernel(
    count, place, source, before, offset, band, value, raw, arrived, field, staged, left
):
    put_first(count, place, source, raw, arrived, before, offset, field, (0, 1, 2, 3, 6, 7, 8, 9))
    side_rows(second_block, field, band, 4, 4, value, staged, left)


def third_kernel(
    count, place, own, side, before, offset, band, value, stats, raw, arrived, field
):
    copies = {}
    for x in (2, 3, 4, 5, 0, 1, 6, 7):
        source = own if 2 <= x < 6 else side
        copies[x] = pltpu.make_async_copy(source.at[x], raw.at[x], arrived.at[x])
        copies[x].start()
    factors = row_factors(before, offset, 16, count * 4 * 32 * 256)
    halve = jnp.where((iota((256, 128), 0) >> 1) == iota((256, 128), 1), 0.125, 0.0).astype(bf16)
    start = place[0] * 2 - 1
    for x in (1, 2, 0, 3):
        copies[2 * x].wait()
        copies[2 * x + 1].wait()
        inside = jnp.logical_and(start + x >= 0, start + x < count * 2)
        field[x, 0:16, :] = jnp.zeros((16, 128), bf16)
        field[x, 272:288, :] = jnp.zeros((16, 128), bf16)
        for group in range(4):
            total = None
            for half in range(2):
                active = normed(raw[2 * x + half, 128 * group : 128 * group + 128, :], factors)
                part = jnp.dot(active.astype(bf16), halve, preferred_element_type=f32)
                total = part if total is None else total + part
            total = jnp.sum(total.reshape(4, 2, 16, 128), axis=1).reshape(64, 128)
            total = jnp.where(inside, total, 0.0).astype(bf16)
            field[x, 16 + 64 * group : 80 + 64 * group, :] = total
    sums = jnp.zeros((32, 128), f32)
    squares = jnp.zeros((32, 128), f32)
    for x in range(2):
        window = jnp.concatenate(
            [
                jnp.concatenate([field[x + dx, 128 * group : 128 * group + 160, :] for dx in range(3)], axis=0)
                for group in range(2)
            ],
            axis=1,
        )
        parts = jnp.dot(band[...], window, preferred_element_type=f32)
        for group in range(2):
            result = merge_depth(parts[:, 128 * group : 128 * group + 128], 256)
            value[x, 256 * group : 256 * group + 256, :] = result
            sums = sums + folded(result, 32)
            squares = squares + folded(result * result, 32)
    put_stats(stats, sums, squares)


def put_middle(count, raw, before, offset, middle, pooled):
    factors = row_factors(before, offset, 32, count * 2 * 16 * 128)
    halve = jnp.where(((iota((64, 512), 1) & 127) >> 1) == iota((64, 512), 0), 0.125, 0.0).astype(bf16)
    for x in range(2):
        for group in range(4):
            active = normed(raw[x, 128 * group : 128 * group + 128, :], factors).astype(bf16)
            middle[x, 128 * group : 128 * group + 128, :] = active
    for part in range(2):
        cells = jnp.concatenate(
            [
                jnp.concatenate(
                    [
                        middle[x, 64 * y + 32 * side : 64 * y + 32 * side + 32, :]
                        for y in range(4 * part, 4 * part + 4)
                    ],
                    axis=0,
                )
                for x in range(2)
                for side in range(2)
            ],
            axis=1,
        )
        total = lax.dot_general(halve, cells, (((1,), (1,)), ((), ())), preferred_element_type=f32)
        pooled[64 * part : 64 * part + 64, :] = total.astype(bf16)


def middle_near_kernel(count, raw, before, offset, own, pooled, middle):
    pooled[0] = own[...]
    put_middle(count, raw, before, offset, middle, pooled.at[1])


def unpacked(pooled):
    pooled = pooled.astype(f32)
    return jnp.concatenate(
        [
            pooled[64 * part : 64 * part + 64, 32 * side : 32 * side + 32]
            for part in range(2)
            for side in range(4)
        ],
        axis=0,
    )


def along_depth(value):
    rows = value.shape[0]
    depth = iota(value.shape, 0) & 63
    before = jnp.where(depth == 0, 0.0, pltpu.roll(value, 1, 0))
    after = jnp.where(depth == 63, 0.0, pltpu.roll(value, rows - 1, 0))
    return before, value, after


def merge_side(parts):
    none = jnp.zeros((64, 128), f32)
    return (
        parts[:, 128:256]
        + jnp.concatenate([none, parts[:-64, 0:128]], axis=0)
        + jnp.concatenate([parts[64:, 256:384], none], axis=0)
    )


def put_lane_stats(stats, result):
    count = stats.shape[0]
    line = jnp.concatenate(
        [jnp.sum(result, axis=0, keepdims=True), jnp.sum(result * result, axis=0, keepdims=True)], axis=0
    )
    stats[...] = jnp.broadcast_to(line[None], (count, 2, 128))


def fourth_taps(kernel, dx):
    return [
        jnp.concatenate([kernel[dx * 9 + dy * 3 + dz] for dy in range(3)], axis=1) for dz in range(3)
    ]


def fourth_row(parts, taps):
    window = jnp.concatenate([view.astype(bf16) for part in parts for view in along_depth(part)], axis=1)
    return merge_side(jnp.dot(window, jnp.concatenate(taps, axis=0), preferred_element_type=f32))


def whole_fourth_row(parts, kernel):
    return fourth_row(parts, [tap for dx in range(3) for tap in fourth_taps(kernel, dx)])


def in_order(place, near, across):
    odd = (place[0] & 1) == 1
    return jnp.where(odd, near, across), jnp.where(odd, across, near)


def side_taps(place, kernel, near):
    odd = (place[0] & 1) == 1
    before, after = fourth_taps(kernel, 0), fourth_taps(kernel, 2)
    pairs = zip(before, after) if near else zip(after, before)
    return [jnp.where(odd, one.astype(f32), other.astype(f32)).astype(bf16) for one, other in pairs]


def fourth_near_kernel(place, pooled, kernel, value):
    taps = fourth_taps(kernel, 1) + side_taps(place, kernel, True)
    value[...] = fourth_row((unpacked(pooled[0]), unpacked(pooled[1])), taps)


def fourth_kernel(place, across, kernel, partial, value, stats, passed):
    result = partial[...] + fourth_row((unpacked(across[0]),), side_taps(place, kernel, False))
    value[...] = result
    put_lane_stats(stats, result)
    passed[...] = across[0]


def fourth_side_kernel(place, pooled, across, kernel_four, kernel, near, side, taps):
    centre, middle, far = unpacked(pooled[0]), unpacked(across[0]), unpacked(across[1])
    low, high = in_order(place, centre, far)
    side[...] = whole_fourth_row((low, middle, high), kernel_four)
    near_taps = fourth_taps(kernel_four, 1) + side_taps(place, kernel_four, False)
    near[...] = fourth_row((unpacked(pooled[1]), centre), near_taps)
    for dx in range(3):
        for dz in range(3):
            row = (dx * 3 + dz) * 128
            for dy in range(3):
                taps[row : row + 128, dy * 128 : dy * 128 + 128] = kernel[dx * 9 + dy * 3 + dz]


def fifth_kernel(
    count, place, passed, near, side, raw, before, offset, kernel_four, taps, value, stats, field
):
    near = near[...] + fourth_row((unpacked(passed[...]),), side_taps(place, kernel_four, True))
    low, high = in_order(place, near, side[...])
    parts = (low, raw[...], high)
    factors = lane_factors(before, offset, count * 8 * 64)
    start = place[0] - 1
    for x, part in enumerate(parts):
        inside = jnp.logical_and(start + x >= 0, start + x < count)
        active = jnp.where(inside, normed(part, factors), 0.0)
        for dz, view in enumerate(along_depth(active)):
            lane = (x * 3 + dz) * 128
            field[:, lane : lane + 128] = view.astype(bf16)
    parts = jnp.dot(field[...], taps[...], preferred_element_type=f32)
    result = merge_side(parts)
    value[...] = result
    put_lane_stats(stats, result)


def decode_kernel(count, place, raw, before, offset, up, middle, decoded):
    factors = lane_factors(before, offset, count * 8 * 64)
    stripe = place[0]
    active = normed(raw[pl.ds(pl.multiple_of(stripe * 64, 64), 64), :], factors).astype(bf16)
    twice = jnp.where((iota((128, 64), 0) >> 1) == iota((128, 64), 1), 1.0, 0.0).astype(bf16)
    active = jnp.dot(twice, active, preferred_element_type=f32).astype(bf16)
    projected = lax.dot_general(up[...], active, (((1,), (1,)), ((), ())), preferred_element_type=f32)
    blocks = []
    for x in range(2):
        own = middle[x, pl.ds(pl.multiple_of(stripe * 64, 64), 64), :].astype(f32)
        for side in range(2):
            merged = jnp.maximum(projected + own[32 * side : 32 * side + 32], 0.0)
            blocks.append(merged.astype(bf16))
    blocks = jnp.concatenate(blocks, axis=0)
    row = iota((128, 128), 0)
    order = jnp.where(((row & 3) * 32 + (row >> 2)) == iota((128, 128), 1), 1.0, 0.0).astype(bf16)
    decoded[...] = jnp.dot(order, blocks, preferred_element_type=f32).astype(bf16)


def shape(dims, kind=f32):
    return jax.ShapeDtypeStruct(dims, kind)


def call(kernel, outs, places, scratch=(), out_places=None, grant=28, flops=1 << 30):
    spaces = {"S": pltpu.SMEM, "V": pltpu.VMEM, "H": pltpu.HBM}

    def specs(letters):
        return tuple(pl.BlockSpec(memory_space=spaces[letter]) for letter in letters)

    single = not isinstance(outs, tuple)
    out_specs = specs(out_places or "V" * (1 if single else len(outs)))
    return pl.pallas_call(
        kernel,
        out_shape=outs,
        in_specs=specs(places),
        out_specs=out_specs[0] if single else out_specs,
        scratch_shapes=list(scratch),
        compiler_params=pltpu.CompilerParams(vmem_limit_bytes=grant * 1024 * 1024),
        cost_estimate=pl.CostEstimate(flops=flops, bytes_accessed=flops >> 8, transcendentals=0),
    )


def swap(stats):
    return lax.all_to_all(stats, "gx", 0, 0)


def bind(kernel, count):
    def bound(*refs):
        kernel(count, *refs)

    return bound


def shards(
    volume,
    weight_one,
    offset_one,
    weight_two,
    offset_two,
    weight_three,
    offset_three,
    weight_four,
    offset_four,
    weight_five,
    offset_five,
    weight_up,
):
    count = lax.axis_size("gx")
    place = lax.axis_index("gx").astype(jnp.int32)[None]
    stripe = lax.axis_index("yz").astype(jnp.int32)[None]

    def swapped(block, first):
        pairs = [(i, i + 1) for i in range(first, count - 1, 2)]
        return lax.ppermute(block, "gx", pairs + [(target, source) for source, target in pairs])

    def line(offset):
        return jnp.pad(offset, (0, 128 - offset.shape[0]))[None]

    statistics = shape((count, 2, 128))
    large, medium, small = 51, 51, 51
    arrivals = pltpu.SemaphoreType.DMA
    block = jnp.transpose(volume, (1, 2, 0, 3)).reshape(4, 16, 256)
    own = lax.all_to_all(jnp.broadcast_to(block[None], (8, 4, 16, 256)), "yz", 0, 0)
    across = swapped(own, 1)
    band_one, band_two, band_three = call(
        bands_kernel,
        (shape((384, 192), bf16), shape((384, 480), bf16), shape((768, 480), bf16)),
        "VVV",
    )(tap_rows(weight_one, 3, 16), tap_rows(weight_two, 0, 10), tap_rows(weight_three, 0, 10))
    near = swapped(own, 0)

    def staged(rows):
        return (pltpu.VMEM((rows, 512, 256), f32), arrivals((rows,)))

    inputs = (place, near, across, own, band_one)
    field = (pltpu.VMEM((12, 160, 256), bf16),)
    partial = call(first_across_kernel, shape((2, 16, 128)), "SVVV", field)(place, across, own, band_one)
    stats = call(first_sums_kernel, statistics, "SVVVV", field, grant=large)(
        place, near, own, band_one, partial
    )
    rows = call(
        first_rows_kernel, shape((10, 512, 256)), "SVVVV", (*field, *staged(10)), "H", large
    )(*inputs)

    inputs = (place, rows, swap(stats), line(offset_one), band_two)
    field = (*staged(10), pltpu.VMEM((10, 544, 256), bf16))
    raw, stats = call(
        bind(second_own_kernel, count),
        (shape((8, 512, 256)), statistics),
        "SHVVV",
        (*field, *staged(4)),
        "HV",
        large,
    )(*inputs)
    side = call(
        bind(second_side_kernel, count),
        shape((8, 512, 256)),
        "SHVVV",
        (*field, *staged(4)),
        "H",
        medium,
    )(*inputs)

    raw, stats = call(
        bind(third_kernel, count),
        (shape((2, 512, 128)), statistics),
        "SHHVVV",
        (*staged(8), pltpu.VMEM((4, 288, 128), bf16)),
        grant=small,
    )(place, raw, side, swap(stats), line(offset_two), band_three)

    near, sums = swapped(raw, 0), swap(stats)
    middle, pooled = call(
        bind(put_middle, count),
        (shape((2, 512, 128), bf16), shape((128, 128), bf16)),
        "VVV",
        flops=1 << 34,
    )(raw, sums, line(offset_three))
    pooled = call(
        bind(middle_near_kernel, count),
        shape((2, 128, 128), bf16),
        "VVVV",
        (pltpu.VMEM((2, 512, 128), bf16),),
    )(near, sums, line(offset_three), pooled)
    across = swapped(pooled, 1)
    taps_four = weight_four.reshape(27, 32, 128)
    taps_five = weight_five.reshape(27, 128, 128)
    partial = call(fourth_near_kernel, shape((512, 128)), "SVV")(place, pooled, taps_four)
    raw, stats, passed = call(
        fourth_kernel,
        (shape((512, 128)), statistics, shape((128, 128), bf16)),
        "SVVV",
    )(place, across, taps_four, partial)
    near, side, taps_five = call(
        fourth_side_kernel, (shape((512, 128)), shape((512, 128)), shape((1152, 384), bf16)), "SVVVV"
    )(place, pooled, across, taps_four, taps_five)
    raw, stats = call(
        bind(fifth_kernel, count),
        (shape((512, 128)), statistics),
        "SVVVVVVVV",
        (pltpu.VMEM((512, 1152), bf16),),
    )(
        place,
        swapped(passed, 0),
        near,
        side,
        raw,
        swap(stats),
        offset_four[None],
        taps_four,
        taps_five,
    )
    decoded = call(
        bind(decode_kernel, count),
        shape((128, 128), bf16),
        "SVVVVV",
    )(stripe, raw, swap(stats), offset_five[None], weight_up.T, middle)
    return decoded.reshape(32, 2, 2, 128)


def solution(mesh):
    return jax.shard_map(
        shards,
        mesh=mesh,
        in_specs=(P(None, "gx", "yz", None), P(), P(), P(), P(), P(), P(), P(), P(), P(), P(), P()),
        out_specs=P(None, "gx", "yz", None),
        check_vma=False,
    )
```
